128 devices in a mesh: det: 4 (over y), tm: 32 (over x, z, core).
Axes of the slice: x: 4, y: 4, z: 4, core: 2. Of those that a mesh axis runs over, the one named last changes fastest.
Arguments:
- timestream: float32 [2048, 16384], P('det', 'tm'), may hold values from -18 to 18
- sample_flags: int32 [2048, 16384], P('det', 'tm'), may hold values 0 or 1
- pointing: bfloat16 [128, 4, 128, 128], P('tm'), may hold values from -0.5 to 0.5
- tile_ids: int32 [128, 4], P('tm'), may hold values from 0 to 127
- block_offsets: int32 [128, 4], P('tm'), may hold values from 0 to 127
- tile_owner: int32 [128], replicated, may hold values from 0 to 127, each once
- det_gains: float32 [2048], P('det'), may hold values from 0.5 to 2
- mode_vectors: float32 [2048, 32], P('det'), may hold values from -0.125 to 0.125
- filter_gain: float32 [257], replicated, may hold values from 0.05 to 1
Outputs:
- tile_snr: float32 [128, 128, 128], P(('det', 'tm'))
- cleaned: bfloat16 [2048, 16384], P('det', 'tm')
The draws below stay inside these ranges and needn't reach their ends.
Inputs may be any that keep to these rules, and one draw needn't show every extreme that they name: Tile t is held in slot tile_owner[t]; slot q belongs to device q of det+tm in mesh order (one tile per device).
All inputs are finite; a program needn't handle non-finite values. No bound on the sum of `sample_flags` on one device may be relied on, other than what follows from the above.
Results may differ from the reference program's by a relative error of at most 0.0085.
Values may be sent and summed in bfloat16 or wider, within the bound.
A program may use at most 64 MiB of HBM per device.

```python
import math
import jax
import jax.numpy as jnp
import numpy as np
from jax import lax

DET_DEV = 512
SAMP_DEV = 512
FLEN = 512
FBINS = 257
SEGLEN = 128
TILE = 128
BLOCKS_TILE = 128
KBLK = 4
MODES = 32
DETS = 2048
SAMPLES = 16384
SEG_DEV = 4
SEGMENTS = 128
NTILES = 128
N_DET = 4
N_TM = 32


def draw_timestream(key, part):
    common_key = jax.random.fold_in(key, 101)
    coupling_key = jax.random.fold_in(key, 202)
    noise_key = jax.random.fold_in(key, 303)
    common = jnp.clip(jax.random.normal(common_key, (SAMPLES,), jnp.float32), -6.0, 6.0)
    coupling = jnp.exp(jax.random.uniform(coupling_key, (DETS,), jnp.float32, math.log(0.5), math.log(2.0)))
    noise = jnp.clip(jax.random.normal(noise_key, (DETS, SAMPLES), jnp.float32), -6.0, 6.0)
    return coupling[:, None] * common[None, :] + noise


def with_ends(values, stream_key, least, largest):
    longest = values.shape.index(max(values.shape))
    spots = []
    for shift in (0, 1):
        where = [jax.random.randint(jax.random.fold_in(stream_key, axis), (), 0, length) for axis, length in enumerate(values.shape)]
        where[longest] = (where[longest] + shift) % values.shape[longest]
        spots.append(tuple(where))
    return values.at[spots[0]].set(least).at[spots[1]].set(largest)


def shard_levels(key, shape, cuts, smallest, high):
    factor_of, own = 1.0, jax.random.fold_in(key, 6)
    for dim, parts in cuts:
        steps = jnp.exp(jax.random.uniform(jax.random.fold_in(own, dim), (parts,), jnp.float32, smallest / len(cuts), high / len(cuts)))
        factor_of = factor_of * jnp.repeat(steps, shape[dim] // parts).reshape([-1 if axis == dim else 1 for axis in range(len(shape))])
    return factor_of


def cumulative_ranks(amount, skew):
    loads = [(1 << 20) // math.isqrt(rank ** skew) + 1 for rank in range(1, amount + 1)]
    deviation = 1 + sum(loads) // (1 << 30)
    return np.cumsum(np.array([max(1, weight // deviation) for weight in loads]))


def skewed_ids(rng, extent, amount, skew):
    listing = cumulative_ranks(amount, skew)
    ticket = jax.random.randint(jax.random.fold_in(rng, 1), extent, 0, int(listing[amount - 1]))
    rank = jnp.searchsorted(jnp.asarray(listing, jnp.int32), ticket, side="right")
    return jax.random.permutation(jax.random.fold_in(rng, 2), amount)[rank].astype(jnp.int32)


def centred(rng, dims, scale, bound, cuts=(), held_as=jnp.bfloat16):
    level = shard_levels(rng, dims, cuts, -0.22, 0.18) if cuts else 1.0
    array = jax.random.normal(rng, dims, jnp.float32) * scale * level
    return jnp.minimum(jnp.maximum(array, -bound), bound).astype(held_as)


def setup_inputs(seed: int = 0) -> dict:
    streams_of = jax.random.split(jax.random.key(seed), 10)
    timestream = draw_timestream(jax.random.fold_in(streams_of[9], 71), 0)
    sample_flags = with_ends((jax.random.randint(streams_of[1], (DETS, SAMPLES), 0, 8) < 1).astype(jnp.int32), jax.random.fold_in(streams_of[1], 1), 0, 1)
    pointing = centred(streams_of[2], (SEGMENTS, KBLK, SEGLEN, TILE), SEGLEN ** -0.5, 0.5, ((0, 32),))
    tile_ids = with_ends(skewed_ids(streams_of[3], (SEGMENTS, KBLK), NTILES, 2), jax.random.fold_in(streams_of[3], 3), 0, NTILES - 1).astype(jnp.int32)
    block_offsets = with_ends(jax.random.randint(streams_of[4], (SEGMENTS, KBLK), 0, BLOCKS_TILE), jax.random.fold_in(streams_of[4], 1), 0, BLOCKS_TILE - 1).astype(jnp.int32)
    tile_owner = jax.random.permutation(streams_of[5], NTILES).astype(jnp.int32)
    det_gains = jnp.clip(jnp.exp(math.log(2.0) - 1.3862944 * jax.random.uniform(streams_of[6], (DETS,), jnp.float32) ** shard_levels(streams_of[6], (DETS,), ((0, 4),), -0.2, 0.2)), 0.5, 2.0)
    mode_vectors = centred(streams_of[7], (DETS, MODES), DETS ** -0.5, 0.125, ((0, 4),), jnp.float32)
    filter_gain = jnp.clip(jnp.exp(jax.random.uniform(streams_of[8], (FBINS,), jnp.float32, math.log(0.05), math.log(1.0))), 0.05, 1.0)
    return dict(timestream=timestream, sample_flags=sample_flags, pointing=pointing, tile_ids=tile_ids, block_offsets=block_offsets, tile_owner=tile_owner, det_gains=det_gains, mode_vectors=mode_vectors, filter_gain=filter_gain)


def spectral_tables():
    position = lax.iota(jnp.int32, FLEN)
    phase_index = position[:, None] * position[None, :] % FLEN
    angles = phase_index.astype(jnp.float32) * (2.0 * math.pi / FLEN)
    return (jnp.cos(angles).astype(jnp.bfloat16), jnp.sin(angles).astype(jnp.bfloat16))

def filter_rows(residual, response, forward, inverse):
    sample_rows = residual.astype(jnp.bfloat16).reshape(-1, FLEN)
    spectrum = jnp.dot(sample_rows, forward, preferred_element_type=jnp.float32)
    shaped = (spectrum * response[None, :]).astype(jnp.bfloat16)
    filtered = jnp.dot(shaped, inverse, preferred_element_type=jnp.float32) / FLEN
    return filtered.reshape(residual.shape)

def reference(timestream, sample_flags, pointing, tile_ids, block_offsets, tile_owner, det_gains, mode_vectors, filter_gain):
    hi = lax.Precision.HIGHEST
    cosine, sine = spectral_tables()
    forward = jnp.concatenate([cosine, sine], axis=1)
    inverse = jnp.concatenate([cosine, sine], axis=0)
    full_gain = jnp.concatenate([filter_gain, filter_gain[1:FLEN // 2][::-1]])
    response = jnp.concatenate([full_gain, full_gain])
    keep = (1 - sample_flags).astype(jnp.float32)
    target_rows = (tile_owner[tile_ids].astype(jnp.int32) * BLOCKS_TILE + block_offsets).reshape(-1).astype(jnp.int32)
    point_float = pointing.astype(jnp.float32)
    squares = lax.optimization_barrier(jnp.sum(point_float * point_float, axis=2))
    weights = (jnp.sum(det_gains * det_gains) * squares).reshape(-1, TILE)
    tod_blocks = timestream.reshape(DETS, N_TM, SAMP_DEV).transpose(1, 0, 2)
    keep_blocks = keep.reshape(DETS, N_TM, SAMP_DEV).transpose(1, 0, 2)
    point_blocks = point_float.reshape(N_TM, SEG_DEV, KBLK, SEGLEN, TILE)
    group_gains = det_gains.reshape(N_DET, DET_DEV)
    total_rows = NTILES * BLOCKS_TILE

    def one_block(inputs):
        tod_part, keep_part, point_part, signal_part = inputs
        residual = (tod_part - det_gains[:, None] * signal_part[None, :]) * keep_part
        filtered = filter_rows(residual, response, forward, inverse)
        amplitudes = jnp.dot(mode_vectors.T, filtered, precision=hi)
        clean = filtered - jnp.dot(mode_vectors, amplitudes, precision=hi)
        summed = jnp.einsum('gd,gds->gs', group_gains, clean.reshape(N_DET, DET_DEV, SAMP_DEV), precision=hi)
        summed = summed.astype(jnp.bfloat16).astype(jnp.float32).reshape(N_DET, SEG_DEV, SEGLEN)
        projected = jnp.einsum('sktp,gst->skp', point_part, summed, precision=hi).reshape(-1, TILE)
        return (projected, clean.astype(jnp.bfloat16))
    zero_signal = jnp.zeros((N_TM, SAMP_DEV), jnp.float32)
    first_proj, unused_clean = lax.map(one_block, (tod_blocks, keep_blocks, point_blocks, zero_signal))
    psum = jnp.zeros((total_rows, TILE), jnp.float32).at[target_rows].add(first_proj.reshape(-1, TILE))
    wsum = jnp.zeros((total_rows, TILE), jnp.float32).at[target_rows].add(weights) + 1.0
    map_rows = psum / wsum
    map_half = map_rows.astype(jnp.bfloat16)
    fetched = map_half[target_rows].astype(jnp.float32).reshape(SEGMENTS, KBLK, TILE)
    signal = jnp.einsum('sktp,skp->st', point_float, fetched, precision=hi).reshape(N_TM, SAMP_DEV)
    second_proj, second_clean = lax.map(one_block, (tod_blocks, keep_blocks, point_blocks, signal))
    psum = jnp.zeros((total_rows, TILE), jnp.float32).at[target_rows].add(second_proj.reshape(-1, TILE))
    map_rows = map_rows + psum / wsum
    tile_snr = (map_rows * jnp.sqrt(wsum)).reshape(NTILES, BLOCKS_TILE, TILE)
    cleaned = second_clean.transpose(1, 0, 2).reshape(DETS, SAMPLES)
    return (tile_snr, cleaned)
```

```python
import functools
import math

import jax
import jax.numpy as jnp
import ml_dtypes
import numpy as np
from jax import lax
from jax.experimental import pallas as pl
from jax.experimental.pallas import tpu as pltpu
from jax.sharding import PartitionSpec as P

FLEN = 512
HALF = FLEN // 2
TILE = 128
SEGLEN = 128
SEG_DEV = 4
KBLK = 4
LISTED = SEG_DEV * KBLK
MODES = 32
F32 = jnp.float32
BF16 = jnp.bfloat16
HI = lax.Precision.HIGHEST
MESH = pl.DeviceIdType.MESH
LAST = (((1,), (1,)), ((), ()))


def half_table():
    position = np.arange(FLEN)
    phase = position[:, None] * position[None, :] % FLEN
    angles = phase.astype(np.float32) * np.float32(2.0 * math.pi / FLEN)
    cosine, sine = np.cos(angles), np.sin(angles)
    table = np.concatenate([cosine[:, : HALF + 1], sine[:, 1:HALF]], axis=1)
    return table.astype(np.float32).astype(ml_dtypes.bfloat16)


def iota(shape, dim):
    return lax.broadcasted_iota(jnp.int32, shape, dim)


def halves(x):
    high = x.astype(BF16).astype(F32)
    return jnp.concatenate([high, x - high], axis=0).astype(BF16)


def folded(y):
    n = y.shape[0] // 2
    return y[:n] + y[n:]


def filter_rows(rows, table, response):
    spectrum = folded(jnp.dot(halves(rows), table, preferred_element_type=F32)) * response
    return folded(lax.dot_general(halves(spectrum), table, LAST, preferred_element_type=F32))


def kernel(
    n_det, n_tm,
    ts_hbm, fl_hbm, pt_hbm, table_hbm, tids, offs, owner, gains, modes, fgain,
    tile_out, clean_hbm,
    ts, fl, pt, table, clean, keepb, vpad, gcol, vcat,
    ubuf, rbuf, kbuf, bkbuf, wbuf, pbuf, qbuf,
    in_sem, out_sem, u_send, u_recv, r_send, r_recv, k_send, k_recv, bk_send, bk_recv,
    w_send, w_recv, p_send, p_recv, q_send, q_recv,
):
    det, tm = lax.axis_index("det"), lax.axis_index("tm")
    listed = n_tm * LISTED

    loads = []
    for n, (src, dst) in enumerate(((ts_hbm, ts), (fl_hbm, fl), (pt_hbm, pt), (table_hbm, table))):
        loads.append(pltpu.make_async_copy(src, dst, in_sem.at[n]))
        loads[-1].start()

    barrier = pltpu.get_barrier_semaphore()
    for d in range(1, n_det):
        pl.semaphore_signal(barrier, inc=1, device_id={"det": lax.rem(det + d, n_det)}, device_id_type=MESH)

    def greet(d, carry):
        pl.semaphore_signal(barrier, inc=1, device_id={"tm": lax.rem(tm + d, n_tm)}, device_id_type=MESH)
        return carry

    lax.fori_loop(1, n_tm, greet, 0)

    def det_copies(buf, send, recv):
        return [
            pltpu.make_async_remote_copy(
                src_ref=buf.at[0], dst_ref=buf.at[d], send_sem=send.at[d - 1], recv_sem=recv.at[d - 1],
                device_id={"det": lax.rem(det + d, n_det)}, device_id_type=MESH,
            )
            for d in range(1, n_det)
        ]

    def start(copies):
        for copy in copies:
            copy.start()

    def arrived(copies):
        for copy in copies:
            copy.wait_recv()

    def spread(buf, send, recv):
        def one(d, carry):
            pltpu.make_async_remote_copy(
                src_ref=buf.at[0], dst_ref=buf.at[d], send_sem=send, recv_sem=recv,
                device_id={"tm": lax.rem(tm + d, n_tm)}, device_id_type=MESH,
            ).start()
            return carry

        lax.fori_loop(1, n_tm, one, 0)

    def all_of(buf, sem):
        rest = buf.at[pl.ds(1, n_tm - 1)]
        pltpu.make_async_copy(rest, rest, sem).wait()

    g = gains[...]
    mode_rows = modes[...]
    vpad[...] = jnp.zeros_like(vpad)
    vpad[:, :MODES] = mode_rows
    vt = vpad[...].T[:MODES]
    ubuf[0] = jnp.zeros((8, 128), F32)
    ubuf[0, :, :MODES] = jnp.dot(
        jnp.broadcast_to(g, (8, g.shape[1])), mode_rows, precision=HI, preferred_element_type=F32
    )
    ubuf[0, :, MODES : 2 * MODES] = jnp.broadcast_to(jnp.sum(g * g, axis=1, keepdims=True), (8, MODES))

    pl.semaphore_wait(barrier, n_det - 1 + n_tm - 1)
    u_copies = det_copies(ubuf, u_send, u_recv)
    start(u_copies)

    first8 = iota((8, FLEN), 0) == 0
    weights = jnp.concatenate([vt, jnp.where(first8, g, 0.0)], axis=0)

    loads[0].wait()
    loads[1].wait()
    keep = (1 - fl[...]).astype(F32)
    keepb[...] = keep.astype(BF16)
    residual = (ts[...] * keep).astype(BF16)
    base = folded(jnp.dot(halves(weights), residual, preferred_element_type=F32))

    arrived(u_copies)
    usum = ubuf[0]
    for d in range(1, n_det):
        usum = usum + ubuf[d]
    u = usum[:, :MODES]
    squared_gain = usum[0:1, MODES : MODES + 1]

    def combine(rows):
        return rows[MODES : MODES + 1] - jnp.dot(u, rows[:MODES], precision=HI, preferred_element_type=F32)[0:1]

    rbuf[0] = combine(base)
    r_copies = det_copies(rbuf, r_send, r_recv)
    start(r_copies)

    loads[2].wait()
    pointing = pt[...].astype(F32)
    squares = jnp.sum((pointing * pointing).reshape(LISTED, SEGLEN, TILE), axis=1)
    lane16 = lax.rem(iota((1, 128), 1), LISTED)
    row16 = iota((LISTED, 128), 0)
    tile_row = jnp.zeros((1, 128), jnp.int32)
    off_row = jnp.zeros((1, 128), jnp.int32)
    own_key = jnp.zeros((LISTED, 128), jnp.int32)
    for n in range(LISTED):
        t, o = tids[n // KBLK, n % KBLK], offs[n // KBLK, n % KBLK]
        tile_row = jnp.where(lane16 == n, t, tile_row)
        off_row = jnp.where(lane16 == n, o, off_row)
        own_key = jnp.where(row16 == n, t * 128 + o, own_key)
    keys = jnp.where(row16 == 0, tile_row.astype(F32), jnp.where(row16 == 1, off_row.astype(F32), 0.0))
    wbuf[0] = jnp.concatenate([squares, keys], axis=0).astype(BF16)
    spread(wbuf, w_send, w_recv)

    kept = folded(jnp.dot(halves(weights * g), keepb[...], preferred_element_type=F32))
    kbuf[0] = combine(kept)
    k_copies = det_copies(kbuf, k_send, k_recv)
    start(k_copies)
    bkbuf[0] = jnp.concatenate([base[:MODES], kept[:MODES]], axis=0).astype(BF16)
    bk_copies = det_copies(bkbuf, bk_send, bk_recv)
    start(bk_copies)

    gain = fgain[...]
    low = gain[:, :HALF]
    lane_half = iota((1, HALF), 1)
    response = jnp.concatenate(
        [
            jnp.where(lane_half == 0, low * (1.0 / FLEN), low * (2.0 / FLEN)),
            jnp.where(lane_half == 0, gain[:, HALF : HALF + 1] * (1.0 / FLEN), low * (2.0 / FLEN)),
        ],
        axis=1,
    )

    def project(z):
        z_high = z.astype(BF16).astype(F32)
        rows = []
        for part in (z_high, z - z_high):
            blocks = []
            for n in range(LISTED):
                s = n // KBLK
                blocks.append(jnp.where(row16 == n, part[:, s * SEGLEN : (s + 1) * SEGLEN], 0.0))
            rows.append(jnp.concatenate(blocks, axis=1))
        lhs = jnp.concatenate(rows, axis=0).astype(BF16)
        return folded(jnp.dot(lhs, pt[...], preferred_element_type=F32))

    loads[3].wait()
    arrived(r_copies)
    r = rbuf[0]
    for d in range(1, n_det):
        r = r + rbuf[d]
    z = filter_rows(jnp.where(first8, r, 0.0), table[...], response)[0:1]
    pbuf[0] = project(z).astype(BF16)
    spread(pbuf, p_send, p_recv)

    gcol[...] = jnp.broadcast_to(g, (128, g.shape[1])).T
    vt_high = vt.astype(BF16).astype(F32)
    vt_low = vt - vt_high
    vcat[...] = jnp.concatenate([vt_high, vt_low, vt_high, jnp.zeros_like(vt)], axis=0).T.astype(BF16)
    all_of(wbuf, w_recv)
    info = wbuf[:, LISTED : 2 * LISTED, :].astype(F32)
    per = 128 // LISTED
    mine = iota((n_tm, LISTED, 128), 2) // LISTED == lax.rem(iota((n_tm, LISTED, 128), 0), per)
    info = jnp.sum(jnp.where(mine, info, 0.0).reshape(n_tm // per, per, LISTED, 128), axis=1)
    key = jnp.concatenate([info[c, 0:1] * 128.0 + info[c, 1:2] for c in range(n_tm // per)], axis=1)
    slot = det * n_tm + tm
    tile_mine = jnp.sum(
        jnp.where(owner[...] == slot, iota((1, 128), 1), 0).astype(F32), axis=1, keepdims=True
    )
    same = (own_key.astype(F32)[:, 0:1] == key).astype(F32).astype(BF16)
    into = (tile_mine * 128.0 + iota((128, listed), 0).astype(F32) == key).astype(F32).astype(BF16)
    all_squares = wbuf[:, :LISTED, :].reshape(listed, TILE)
    own_weight = 1.0 + squared_gain * jnp.dot(same, all_squares, preferred_element_type=F32)
    tile_weight = 1.0 + squared_gain * jnp.dot(into, all_squares, preferred_element_type=F32)
    arrived(k_copies)
    arrived(bk_copies)
    k = kbuf[0]
    bk = bkbuf[0].astype(F32)
    for d in range(1, n_det):
        k = k + kbuf[d]
        bk = bk + bkbuf[d].astype(F32)

    all_of(pbuf, p_recv)
    first = pbuf[...].reshape(listed, TILE)
    fetched = (jnp.dot(same, first, preferred_element_type=F32) / own_weight).astype(BF16)
    wide = lax.dot_general(fetched, pt[...], LAST, preferred_element_type=F32)
    diagonal = iota((LISTED, LISTED * SEGLEN), 0) == iota((LISTED, LISTED * SEGLEN), 1) // SEGLEN
    flat = jnp.sum(jnp.where(diagonal, wide, 0.0), axis=0, keepdims=True)
    parts = []
    for s in range(SEG_DEV):
        total = flat[:, s * KBLK * SEGLEN : (s * KBLK + 1) * SEGLEN]
        for n in range(s * KBLK + 1, (s + 1) * KBLK):
            total = total + flat[:, n * SEGLEN : (n + 1) * SEGLEN]
        parts.append(total)
    sig = jnp.concatenate(parts, axis=1)

    rows = jnp.concatenate([bk[:MODES] - sig * bk[MODES:], jnp.where(first8, r - sig * k, 0.0)], axis=0)
    rows = filter_rows(rows, table[...], response)
    qbuf[0] = project(rows[MODES : MODES + 1]).astype(BF16)
    spread(qbuf, q_send, q_recv)

    amp = rows[:MODES]
    amp_high = amp.astype(BF16).astype(F32)
    amp_cat = jnp.concatenate([amp_high, amp_high, amp - amp_high, jnp.zeros_like(amp)], axis=0).astype(BF16)
    chunk = 128

    def clean_rows(c, carry):
        at = pl.ds(pl.multiple_of(c * chunk, chunk), chunk)
        gains_here = jnp.concatenate([gcol[at, :]] * (FLEN // 128), axis=1)
        left = ((ts[at, :] - gains_here * sig) * keepb[at, :].astype(F32)).astype(BF16)
        shaped = (jnp.dot(left, table[...], preferred_element_type=F32) * response).astype(BF16)
        filtered = lax.dot_general(shaped, table[...], LAST, preferred_element_type=F32)
        filtered = filtered - jnp.dot(vcat[at, :], amp_cat, preferred_element_type=F32)
        clean[at, :] = filtered.astype(BF16)
        return carry

    lax.fori_loop(0, ts.shape[0] // chunk, clean_rows, 0)
    out = pltpu.make_async_copy(clean, clean_hbm, out_sem)
    out.start()
    sums = jnp.dot(into, first, preferred_element_type=F32) / tile_weight

    all_of(qbuf, q_recv)
    second = qbuf[...].reshape(listed, TILE)
    sums = sums + jnp.dot(into, second, preferred_element_type=F32) / tile_weight
    tile_out[...] = sums * jnp.sqrt(tile_weight)

    for copies in (u_copies, r_copies, k_copies, bk_copies):
        for copy in copies:
            copy.wait_send()
    all_of(wbuf, w_send)
    all_of(pbuf, p_send)
    all_of(qbuf, q_send)
    out.wait()


def solution(mesh):
    n_det, n_tm = mesh.shape["det"], mesh.shape["tm"]
    table_const = half_table()

    def shards(
        timestream, sample_flags, pointing, tile_ids, block_offsets, tile_owner, det_gains, mode_vectors, filter_gain
    ):
        dets, samples = timestream.shape
        anywhere = pl.BlockSpec(memory_space=pl.ANY)
        vmem = pl.BlockSpec(memory_space=pltpu.VMEM)
        smem = pl.BlockSpec(memory_space=pltpu.SMEM)
        dma = pltpu.SemaphoreType.DMA
        tile_snr, cleaned = pl.pallas_call(
            functools.partial(kernel, n_det, n_tm),
            out_shape=(
                jax.ShapeDtypeStruct((TILE, TILE), F32),
                jax.ShapeDtypeStruct((dets, samples), BF16),
            ),
            in_specs=[anywhere] * 4 + [smem] * 2 + [vmem] * 4,
            out_specs=(vmem, anywhere),
            scratch_shapes=[
                pltpu.VMEM((dets, samples), F32),
                pltpu.VMEM((dets, samples), jnp.int32),
                pltpu.VMEM((LISTED * SEGLEN, TILE), BF16),
                pltpu.VMEM((FLEN, FLEN), BF16),
                pltpu.VMEM((dets, samples), BF16),
                pltpu.VMEM((dets, samples), BF16),
                pltpu.VMEM((dets, 128), F32),
                pltpu.VMEM((dets, 128), F32),
                pltpu.VMEM((dets, 128), BF16),
                pltpu.VMEM((n_det, 8, 128), F32),
                pltpu.VMEM((n_det, 1, samples), F32),
                pltpu.VMEM((n_det, 1, samples), F32),
                pltpu.VMEM((n_det, 2 * MODES, samples), BF16),
                pltpu.VMEM((n_tm, 2 * LISTED, TILE), BF16),
                pltpu.VMEM((n_tm, LISTED, TILE), BF16),
                pltpu.VMEM((n_tm, LISTED, TILE), BF16),
                dma((4,)),
                dma,
            ]
            + [dma((n_det - 1,))] * 8
            + [dma] * 6,
            compiler_params=pltpu.CompilerParams(
                collective_id=0, has_side_effects=True, vmem_limit_bytes=40 * 1024 * 1024
            ),
        )(
            timestream,
            sample_flags,
            pointing.reshape(LISTED * SEGLEN, TILE),
            jnp.asarray(table_const),
            tile_ids,
            block_offsets,
            tile_owner.reshape(1, -1),
            det_gains.reshape(1, -1),
            mode_vectors,
            filter_gain.reshape(1, -1),
        )
        return tile_snr.reshape(1, TILE, TILE), cleaned

    return jax.shard_map(
        shards,
        mesh=mesh,
        in_specs=(
            P("det", "tm"), P("det", "tm"), P("tm", None, None, None), P("tm", None), P("tm", None),
            P(), P("det"), P("det", None), P(),
        ),
        out_specs=(P(("det", "tm"), None, None), P("det", "tm")),
        check_vma=False,
    )
```

```python
import functools
import math

import jax
import jax.numpy as jnp
import ml_dtypes
import numpy as np
from jax import lax
from jax.experimental import pallas as pl
from jax.experimental.pallas import tpu as pltpu
from jax.sharding import PartitionSpec as P

FLEN = 512
HALF = FLEN // 2
TILE = 128
SEGLEN = 128
SEG_DEV = 4
KBLK = 4
LISTED = SEG_DEV * KBLK
MODES = 32
F32 = jnp.float32
BF16 = jnp.bfloat16
HI = lax.Precision.HIGHEST
MESH = pl.DeviceIdType.MESH
LAST = (((1,), (1,)), ((), ()))


def half_table():
    position = np.arange(FLEN)
    phase = position[:, None] * position[None, :] % FLEN
    angles = phase.astype(np.float32) * np.float32(2.0 * math.pi / FLEN)
    cosine, sine = np.cos(angles), np.sin(angles)
    table = np.concatenate([cosine[:, : HALF + 1], sine[:, 1:HALF]], axis=1)
    return table.astype(np.float32).astype(ml_dtypes.bfloat16)


def iota(shape, dim):
    return lax.broadcasted_iota(jnp.int32, shape, dim)


def halves(x):
    high = x.astype(BF16).astype(F32)
    return jnp.concatenate([high, x - high], axis=0).astype(BF16)


def folded(y):
    n = y.shape[0] // 2
    return y[:n] + y[n:]


def kernel(
    n_det, n_tm,
    gains_hbm, modes_hbm, fl_hbm, ts_hbm, pt_hbm, tids_hbm, offs_hbm, table_hbm, fgain_hbm, owner_hbm,
    tile_out, clean,
    gains, modes, fl, ts, pt, tids, offs, table, fgain, owner,
    keepb, gcol, vcat, table_t, pt_t, wide_filter,
    ybuf, xbuf, lbuf, kbuf, wbuf, pbuf, qbuf,
    in_sem, y_send, y_recv, x_send, x_recv, l_send, l_recv, k_send, k_recv,
    w_send, w_recv, p_send, p_recv, q_send, q_recv,
):
    det, tm = lax.axis_index("det"), lax.axis_index("tm")
    listed = n_tm * LISTED

    loads = []
    pairs = (
        (gains_hbm, gains), (modes_hbm, modes), (fl_hbm, fl), (ts_hbm, ts), (pt_hbm, pt),
        (tids_hbm, tids), (offs_hbm, offs), (table_hbm, table), (fgain_hbm, fgain), (owner_hbm, owner),
    )
    for n, (src, dst) in enumerate(pairs):
        loads.append(pltpu.make_async_copy(src, dst, in_sem.at[n]))
        loads[-1].start()

    n_z = 4
    n_x = n_tm // (2 * n_z)
    tm_x, tm_z, tm_core = tm // (2 * n_z), lax.rem(tm // 2, n_z), lax.rem(tm, 2)
    offsets = [(dx, dz, dc) for dx in range(n_x) for dz in range(n_z) for dc in range(2) if dx or dz or dc]
    offsets.sort(key=lambda o: -(min(o[0], n_x - o[0]) * 10 + min(o[1], n_z - o[1]) * 10 + o[2]))
    peers = []
    for dx, dz, dc in offsets:
        peer = (
            lax.rem(tm_x + dx, n_x) * (2 * n_z) + lax.rem(tm_z + dz, n_z) * 2 + lax.rem(tm_core + dc, 2)
        )
        peers.append((dx * 2 * n_z + dz * 2 + dc, {"tm": peer}))
    det_peers = [{"det": lax.rem(det + d, n_det)} for d in range(1, n_det)]

    barrier = pltpu.get_barrier_semaphore()
    for _, peer in peers:
        pl.semaphore_signal(barrier, inc=1, device_id=peer, device_id_type=MESH)
    for peer in det_peers:
        pl.semaphore_signal(barrier, inc=1, device_id=peer, device_id_type=MESH)

    def det_copies(buf, send, recv):
        return [
            pltpu.make_async_remote_copy(
                src_ref=buf.at[0], dst_ref=buf.at[d], send_sem=send.at[d - 1], recv_sem=recv.at[d - 1],
                device_id=det_peers[d - 1], device_id_type=MESH,
            )
            for d in range(1, n_det)
        ]

    def start(copies):
        for copy in copies:
            copy.start()

    def arrived(copies):
        for copy in copies:
            copy.wait_recv()

    def spread(buf, send, recv):
        for d, peer in peers:
            pltpu.make_async_remote_copy(
                src_ref=buf.at[0], dst_ref=buf.at[d], send_sem=send, recv_sem=recv,
                device_id=peer, device_id_type=MESH,
            ).start()

    def all_of(buf, sem):
        rest = buf.at[pl.ds(1, n_tm - 1)]
        pltpu.make_async_copy(rest, rest, sem).wait()

    loads[0].wait()
    loads[1].wait()
    g = gains[...]
    vt = modes[...]
    copies_u = jnp.concatenate(
        [lax.dot_general(jnp.broadcast_to(g, (8, g.shape[1])), vt, LAST, precision=HI, preferred_element_type=F32)]
        * n_det,
        axis=1,
    )[0:1]
    squared = jnp.broadcast_to(jnp.sum(g * g, axis=1, keepdims=True), (1, FLEN - n_det * MODES))
    first8 = iota((8, FLEN), 0) == 0
    weights = jnp.concatenate([vt, jnp.where(first8, g, 0.0)], axis=0)
    weight_halves = halves(weights)

    loads[2].wait()
    loads[3].wait()
    keep = (1 - fl[...]).astype(F32)
    keepb[...] = keep.astype(BF16)
    residual = (ts[...] * keep).astype(BF16)
    base = folded(jnp.dot(weight_halves, residual, preferred_element_type=F32))
    xbuf[0] = base[:MODES].astype(BF16)
    ybuf[0] = jnp.concatenate([base[MODES : MODES + 1], jnp.concatenate([copies_u, squared], axis=1)], axis=0)
    pl.semaphore_wait(barrier, n_det - 1 + n_tm - 1)
    x_copies = det_copies(xbuf, x_send, x_recv)
    y_copies = det_copies(ybuf, y_send, y_recv)
    start(x_copies)
    start(y_copies)

    for n in (4, 5, 6):
        loads[n].wait()
    pointing = pt[...].astype(F32)
    squares = jnp.sum((pointing * pointing).reshape(LISTED, SEGLEN, TILE), axis=1)
    lane16 = lax.rem(iota((1, 128), 1), LISTED)
    row16 = iota((LISTED, 128), 0)
    tile_row = jnp.zeros((1, 128), jnp.int32)
    off_row = jnp.zeros((1, 128), jnp.int32)
    own_key = jnp.zeros((LISTED, 128), jnp.int32)
    for n in range(LISTED):
        t, o = tids[n // KBLK, n % KBLK], offs[n // KBLK, n % KBLK]
        tile_row = jnp.where(lane16 == n, t, tile_row)
        off_row = jnp.where(lane16 == n, o, off_row)
        own_key = jnp.where(row16 == n, t * 128 + o, own_key)
    keys = jnp.where(row16 == 0, tile_row.astype(F32), jnp.where(row16 == 1, off_row.astype(F32), 0.0))
    wbuf[0] = jnp.concatenate([squares, keys], axis=0).astype(BF16)
    spread(wbuf, w_send, w_recv)

    kept = folded(jnp.dot(halves(weights * g), keepb[...], preferred_element_type=F32))
    lbuf[0] = kept[:MODES].astype(BF16)
    kbuf[0] = kept[MODES : MODES + 1]
    l_copies = det_copies(lbuf, l_send, l_recv)
    k_copies = det_copies(kbuf, k_send, k_recv)
    start(l_copies)
    start(k_copies)

    loads[8].wait()
    gain = fgain[...].reshape(1, HALF + 1)
    low = gain[:, :HALF]
    lane_half = iota((1, HALF), 1)
    response = jnp.concatenate(
        [
            jnp.where(lane_half == 0, low * (1.0 / FLEN), low * (2.0 / FLEN)),
            jnp.where(lane_half == 0, gain[:, HALF : HALF + 1] * (1.0 / FLEN), low * (2.0 / FLEN)),
        ],
        axis=1,
    )
    loads[7].wait()
    table_t[...] = table[...].T
    scaled = table[...].astype(F32) * response
    scaled_high = scaled.astype(BF16)
    scaled_low = (scaled - scaled_high.astype(F32)).astype(BF16)
    whole = jnp.dot(scaled_high, table_t[...], preferred_element_type=F32)
    whole = whole + jnp.dot(scaled_low, table_t[...], preferred_element_type=F32)
    whole_high = whole.astype(BF16)
    wide_filter[:, :FLEN] = whole_high
    wide_filter[:, FLEN:] = (whole - whole_high.astype(F32)).astype(BF16)

    def filter_rows(rows):
        both = jnp.dot(halves(rows), wide_filter[...], preferred_element_type=F32)
        n = rows.shape[0]
        return both[:n, :FLEN] + both[n:, :FLEN] + both[:n, FLEN:]

    def project(z):
        z_high = z.astype(BF16).astype(F32)
        rows = []
        for part in (z_high, z - z_high):
            blocks = []
            for n in range(LISTED):
                s = n // KBLK
                blocks.append(jnp.where(row16 == n, part[:, s * SEGLEN : (s + 1) * SEGLEN], 0.0))
            rows.append(jnp.concatenate(blocks, axis=1))
        lhs = jnp.concatenate(rows, axis=0).astype(BF16)
        return folded(jnp.dot(lhs, pt[...], preferred_element_type=F32))

    arrived(x_copies)
    arrived(y_copies)
    y = ybuf[0]
    for d in range(1, n_det):
        y = y + ybuf[d]
    u = halves(jnp.broadcast_to(y[1:2, : n_det * MODES], (8, n_det * MODES)))
    squared_gain = y[1:2, FLEN - 1 : FLEN]

    def combine(total, group_rows):
        return total - folded(
            jnp.dot(u, group_rows[...].reshape(n_det * MODES, FLEN), preferred_element_type=F32)
        )

    r = combine(y[0:1], xbuf)
    pbuf[0] = project(filter_rows(r)[0:1]).astype(BF16)
    spread(pbuf, p_send, p_recv)

    for n in range(LISTED):
        pt_t[:, n * SEGLEN : (n + 1) * SEGLEN] = pt[n * SEGLEN : (n + 1) * SEGLEN, :].T
    gcol[...] = jnp.broadcast_to(g, (128, g.shape[1])).T
    vt_high = vt.astype(BF16).astype(F32)
    vt_low = vt - vt_high
    vcat[...] = jnp.concatenate([vt_high, vt_low, vt_high, jnp.zeros_like(vt)], axis=0).T.astype(BF16)
    arrived(l_copies)
    arrived(k_copies)
    k = kbuf[0]
    base_sum = xbuf[0].astype(F32)
    kept_sum = lbuf[0].astype(F32)
    for d in range(1, n_det):
        k = k + kbuf[d]
        base_sum = base_sum + xbuf[d].astype(F32)
        kept_sum = kept_sum + lbuf[d].astype(F32)
    k = combine(k, lbuf)
    all_of(wbuf, w_recv)
    info = wbuf[:, LISTED : 2 * LISTED, :].astype(F32)
    per = 128 // LISTED
    mine = iota((n_tm, LISTED, 128), 2) // LISTED == lax.rem(iota((n_tm, LISTED, 128), 0), per)
    info = jnp.sum(jnp.where(mine, info, 0.0).reshape(n_tm // per, per, LISTED, 128), axis=1)
    key = jnp.concatenate([info[c, 0:1] * 128.0 + info[c, 1:2] for c in range(n_tm // per)], axis=1)
    slot = det * n_tm + tm
    loads[9].wait()
    tile_mine = jnp.sum(
        jnp.where(owner[...] == slot, iota((1, 128), 1), 0).astype(F32), axis=1, keepdims=True
    )
    same = (own_key.astype(F32)[:, 0:1] == key).astype(F32).astype(BF16)
    into = (tile_mine * 128.0 + iota((128, listed), 0).astype(F32) == key).astype(F32).astype(BF16)
    all_squares = wbuf[:, :LISTED, :].reshape(listed, TILE)
    own_scale = 1.0 / (1.0 + squared_gain * jnp.dot(same, all_squares, preferred_element_type=F32))
    tile_weight = 1.0 + squared_gain * jnp.dot(into, all_squares, preferred_element_type=F32)
    tile_scale = jnp.sqrt(tile_weight) / tile_weight

    all_of(pbuf, p_recv)
    first = pbuf[...].reshape(listed, TILE)
    fetched = (jnp.dot(same, first, preferred_element_type=F32) * own_scale).astype(BF16)
    wide = jnp.dot(fetched, pt_t[...], preferred_element_type=F32)
    diagonal = iota((LISTED, LISTED * SEGLEN), 0) == iota((LISTED, LISTED * SEGLEN), 1) // SEGLEN
    flat = jnp.sum(jnp.where(diagonal, wide, 0.0), axis=0, keepdims=True)
    parts = []
    for s in range(SEG_DEV):
        total = flat[:, s * KBLK * SEGLEN : (s * KBLK + 1) * SEGLEN]
        for n in range(s * KBLK + 1, (s + 1) * KBLK):
            total = total + flat[:, n * SEGLEN : (n + 1) * SEGLEN]
        parts.append(total)
    sig = jnp.concatenate(parts, axis=1)
    qbuf[0] = project(filter_rows(r - sig * k)[0:1]).astype(BF16)
    spread(qbuf, q_send, q_recv)

    amp = filter_rows(base_sum - sig * kept_sum)
    amp_high = amp.astype(BF16).astype(F32)
    amp_cat = jnp.concatenate([amp_high, amp_high, amp - amp_high, jnp.zeros_like(amp)], axis=0).astype(BF16)
    chunk = 128

    def clean_rows(c, carry):
        at = pl.ds(pl.multiple_of(c * chunk, chunk), chunk)
        gains_here = jnp.concatenate([gcol[at, :]] * (FLEN // 128), axis=1)
        left = ((ts[at, :] - gains_here * sig) * keepb[at, :].astype(F32)).astype(BF16)
        shaped = (jnp.dot(left, table[...], preferred_element_type=F32) * response).astype(BF16)
        filtered = jnp.dot(shaped, table_t[...], preferred_element_type=F32)
        filtered = filtered - jnp.dot(vcat[at, :], amp_cat, preferred_element_type=F32)
        clean[at, :] = filtered.astype(BF16)
        return carry

    lax.fori_loop(0, ts.shape[0] // chunk, clean_rows, 0)
    sums = jnp.dot(into, first, preferred_element_type=F32)

    all_of(qbuf, q_recv)
    second = qbuf[...].reshape(listed, TILE)
    sums = sums + jnp.dot(into, second, preferred_element_type=F32)
    tile_out[...] = sums * tile_scale

    for copies in (x_copies, y_copies, l_copies, k_copies):
        for copy in copies:
            copy.wait_send()
    all_of(wbuf, w_send)
    all_of(pbuf, p_send)
    all_of(qbuf, q_send)


def solution(mesh):
    n_det, n_tm = mesh.shape["det"], mesh.shape["tm"]
    table_const = half_table()

    def shards(
        timestream, sample_flags, pointing, tile_ids, block_offsets, tile_owner, det_gains, mode_vectors, filter_gain
    ):
        dets, samples = timestream.shape
        hbm = pl.BlockSpec(memory_space=pltpu.HBM)
        vmem = pl.BlockSpec(memory_space=pltpu.VMEM)
        dma = pltpu.SemaphoreType.DMA
        tile_snr, cleaned = pl.pallas_call(
            functools.partial(kernel, n_det, n_tm),
            out_shape=(
                jax.ShapeDtypeStruct((TILE, TILE), F32),
                jax.ShapeDtypeStruct((dets, samples), BF16),
            ),
            in_specs=[hbm] * 10,
            out_specs=(vmem, vmem),
            scratch_shapes=[
                pltpu.VMEM((1, dets), F32),
                pltpu.VMEM((MODES, dets), F32),
                pltpu.VMEM((dets, samples), jnp.int32),
                pltpu.VMEM((dets, samples), F32),
                pltpu.VMEM((LISTED * SEGLEN, TILE), BF16),
                pltpu.SMEM((SEG_DEV, KBLK), jnp.int32),
                pltpu.SMEM((SEG_DEV, KBLK), jnp.int32),
                pltpu.VMEM((FLEN, FLEN), BF16),
                pltpu.VMEM((HALF + 1,), F32),
                pltpu.VMEM((1, tile_owner.shape[0]), jnp.int32),
                pltpu.VMEM((dets, samples), BF16),
                pltpu.VMEM((dets, 128), F32),
                pltpu.VMEM((dets, 128), BF16),
                pltpu.VMEM((FLEN, FLEN), BF16),
                pltpu.VMEM((TILE, LISTED * SEGLEN), BF16),
                pltpu.VMEM((FLEN, 2 * FLEN), BF16),
                pltpu.VMEM((n_det, 2, samples), F32),
                pltpu.VMEM((n_det, MODES, samples), BF16),
                pltpu.VMEM((n_det, MODES, samples), BF16),
                pltpu.VMEM((n_det, 1, samples), F32),
                pltpu.VMEM((n_tm, 2 * LISTED, TILE), BF16),
                pltpu.VMEM((n_tm, LISTED, TILE), BF16),
                pltpu.VMEM((n_tm, LISTED, TILE), BF16),
                dma((10,)),
            ]
            + [dma((n_det - 1,))] * 8
            + [dma] * 6,
            compiler_params=pltpu.CompilerParams(
                collective_id=0, has_side_effects=True, vmem_limit_bytes=40 * 1024 * 1024
            ),
        )(
            *(
                pltpu.with_memory_space_constraint(operand, pltpu.HBM)
                for operand in (
                    det_gains.reshape(1, -1),
                    mode_vectors.T,
                    sample_flags,
                    timestream,
                    pointing.reshape(LISTED * SEGLEN, TILE),
                    tile_ids,
                    block_offsets,
                    jnp.asarray(table_const),
                    filter_gain,
                    tile_owner.reshape(1, -1),
                )
            )
        )
        return tile_snr.reshape(1, TILE, TILE), cleaned

    return jax.shard_map(
        shards,
        mesh=mesh,
        in_specs=(
            P("det", "tm"), P("det", "tm"), P("tm", None, None, None), P("tm", None), P("tm", None),
            P(), P("det"), P("det", None), P(),
        ),
        out_specs=(P(("det", "tm"), None, None), P("det", "tm")),
        check_vma=False,
    )
```

```python
import functools
import math

import jax
import jax.numpy as jnp
import ml_dtypes
import numpy as np
from jax import lax
from jax.experimental import pallas as pl
from jax.experimental.pallas import tpu as pltpu
from jax.sharding import PartitionSpec as P

FLEN = 512
HALF = FLEN // 2
TILE = 128
SEGLEN = 128
SEG_DEV = 4
KBLK = 4
LISTED = SEG_DEV * KBLK
MODES = 32
F32 = jnp.float32
BF16 = jnp.bfloat16
HI = lax.Precision.HIGHEST
MESH = pl.DeviceIdType.MESH
LAST = (((1,), (1,)), ((), ()))


def half_table():
    position = np.arange(FLEN)
    phase = position[:, None] * position[None, :] % FLEN
    angles = phase.astype(np.float32) * np.float32(2.0 * math.pi / FLEN)
    cosine, sine = np.cos(angles), np.sin(angles)
    table = np.concatenate([cosine[:, : HALF + 1], sine[:, 1:HALF]], axis=1)
    return table.astype(np.float32).astype(ml_dtypes.bfloat16)


def iota(shape, dim):
    return lax.broadcasted_iota(jnp.int32, shape, dim)


def halves(x):
    high = x.astype(BF16).astype(F32)
    return jnp.concatenate([high, x - high], axis=0).astype(BF16)


def folded(y):
    n = y.shape[0] // 2
    return y[:n] + y[n:]


def kernel(
    n_det, n_tm,
    gains_hbm, modes_hbm, fl_hbm, ts_hbm, pt_hbm, tids_hbm, offs_hbm, table_hbm, fgain_hbm, owner_hbm,
    tile_out, clean,
    gains, modes, fl, ts, pt, tids, offs, table, fgain, owner,
    keepb, gcol, vcat, table_t, pt_t, wide_filter,
    ybuf, xbuf, lbuf, kbuf, wbuf, pbuf, qbuf,
    column_sem, in_sem, y_send, y_recv, x_send, x_recv, l_send, l_recv, k_send, k_recv,
    w_send, w_recv, p_send, p_recv, q_send, q_recv,
):
    det, tm = lax.axis_index("det"), lax.axis_index("tm")
    listed = n_tm * LISTED

    loads = []
    pairs = (
        (gains_hbm, gains), (modes_hbm, modes), (fl_hbm, fl), (ts_hbm, ts), (pt_hbm, pt),
        (tids_hbm, tids), (offs_hbm, offs), (table_hbm, table), (fgain_hbm, fgain), (owner_hbm, owner),
    )
    for n, (src, dst) in enumerate(pairs):
        loads.append(pltpu.make_async_copy(src, dst, in_sem.at[n]))
        loads[-1].start()

    n_z = 4
    n_x = n_tm // (2 * n_z)
    tm_x, tm_z, tm_core = tm // (2 * n_z), lax.rem(tm // 2, n_z), lax.rem(tm, 2)
    offsets = [(dx, dz, dc) for dx in range(n_x) for dz in range(n_z) for dc in range(2) if dx or dz or dc]
    offsets.sort(key=lambda o: -(min(o[0], n_x - o[0]) * 10 + min(o[1], n_z - o[1]) * 10 + o[2]))
    peers = []
    for dx, dz, dc in offsets:
        peer = (
            lax.rem(tm_x + dx, n_x) * (2 * n_z) + lax.rem(tm_z + dz, n_z) * 2 + lax.rem(tm_core + dc, 2)
        )
        peers.append((dx * 2 * n_z + dz * 2 + dc, {"tm": peer}))
    det_peers = [{"det": lax.rem(det + d, n_det)} for d in range(1, n_det)]

    barrier = pltpu.get_barrier_semaphore()
    row_peers = [peer for (dx, dz, dc), (_, peer) in zip(offsets, peers) if dz == 0 and dc == 0]
    column_peers = [peer for (dx, dz, dc), (_, peer) in zip(offsets, peers) if dx == 0]
    near = det_peers + row_peers + column_peers
    for peer in near:
        pl.semaphore_signal(barrier, inc=1, device_id=peer, device_id_type=MESH)

    def det_copies(buf, send, recv):
        return [
            pltpu.make_async_remote_copy(
                src_ref=buf.at[0], dst_ref=buf.at[d], send_sem=send.at[d - 1], recv_sem=recv.at[d - 1],
                device_id=det_peers[d - 1], device_id_type=MESH,
            )
            for d in range(1, n_det)
        ]

    def start(copies):
        for copy in copies:
            copy.start()

    def arrived(copies):
        for copy in copies:
            copy.wait_recv()

    def spread(buf, send, recv):
        for d, peer in peers:
            pltpu.make_async_remote_copy(
                src_ref=buf.at[0], dst_ref=buf.at[d], send_sem=send, recv_sem=recv,
                device_id=peer, device_id_type=MESH,
            ).start()

    def all_of(buf, sem):
        rest = buf.at[pl.ds(1, n_tm - 1)]
        pltpu.make_async_copy(rest, rest, sem).wait()

    loads[0].wait()
    loads[1].wait()
    g = gains[...]
    vt = modes[...]
    copies_u = jnp.concatenate(
        [lax.dot_general(jnp.broadcast_to(g, (8, g.shape[1])), vt, LAST, precision=HI, preferred_element_type=F32)]
        * n_det,
        axis=1,
    )[0:1]
    squared = jnp.broadcast_to(jnp.sum(g * g, axis=1, keepdims=True), (1, FLEN - n_det * MODES))
    first8 = iota((8, FLEN), 0) == 0
    weights = jnp.concatenate([vt, jnp.where(first8, g, 0.0)], axis=0)
    weight_halves = halves(weights)

    loads[2].wait()
    loads[3].wait()
    keep = (1 - fl[...]).astype(F32)
    keepb[...] = keep.astype(BF16)
    residual = (ts[...] * keep).astype(BF16)
    base = folded(jnp.dot(weight_halves, residual, preferred_element_type=F32))
    xbuf[0] = base[:MODES].astype(BF16)
    ybuf[0] = jnp.concatenate([base[MODES : MODES + 1], jnp.concatenate([copies_u, squared], axis=1)], axis=0)
    pl.semaphore_wait(barrier, len(near))
    for peer in row_peers:
        pl.semaphore_signal(column_sem, inc=1, device_id=peer, device_id_type=MESH)
    x_copies = det_copies(xbuf, x_send, x_recv)
    y_copies = det_copies(ybuf, y_send, y_recv)
    start(x_copies)
    start(y_copies)

    for n in (4, 5, 6):
        loads[n].wait()
    pointing = pt[...].astype(F32)
    squares = jnp.sum((pointing * pointing).reshape(LISTED, SEGLEN, TILE), axis=1)
    lane16 = lax.rem(iota((1, 128), 1), LISTED)
    row16 = iota((LISTED, 128), 0)
    tile_row = jnp.zeros((1, 128), jnp.int32)
    off_row = jnp.zeros((1, 128), jnp.int32)
    own_key = jnp.zeros((LISTED, 128), jnp.int32)
    for n in range(LISTED):
        t, o = tids[n // KBLK, n % KBLK], offs[n // KBLK, n % KBLK]
        tile_row = jnp.where(lane16 == n, t, tile_row)
        off_row = jnp.where(lane16 == n, o, off_row)
        own_key = jnp.where(row16 == n, t * 128 + o, own_key)
    keys = jnp.where(row16 == 0, tile_row.astype(F32), jnp.where(row16 == 1, off_row.astype(F32), 0.0))
    wbuf[0] = jnp.concatenate([squares, keys], axis=0).astype(BF16)
    pl.semaphore_wait(column_sem, len(row_peers))
    spread(wbuf, w_send, w_recv)

    kept = folded(jnp.dot(halves(weights * g), keepb[...], preferred_element_type=F32))
    lbuf[0] = kept[:MODES].astype(BF16)
    kbuf[0] = kept[MODES : MODES + 1]
    l_copies = det_copies(lbuf, l_send, l_recv)
    k_copies = det_copies(kbuf, k_send, k_recv)
    start(l_copies)
    start(k_copies)

    loads[8].wait()
    gain = fgain[...].reshape(1, HALF + 1)
    low = gain[:, :HALF]
    lane_half = iota((1, HALF), 1)
    response = jnp.concatenate(
        [
            jnp.where(lane_half == 0, low * (1.0 / FLEN), low * (2.0 / FLEN)),
            jnp.where(lane_half == 0, gain[:, HALF : HALF + 1] * (1.0 / FLEN), low * (2.0 / FLEN)),
        ],
        axis=1,
    )
    loads[7].wait()
    table_t[...] = table[...].T
    scaled = table[...].astype(F32) * response
    scaled_high = scaled.astype(BF16)
    scaled_low = (scaled - scaled_high.astype(F32)).astype(BF16)
    whole = jnp.dot(scaled_high, table_t[...], preferred_element_type=F32)
    whole = whole + jnp.dot(scaled_low, table_t[...], preferred_element_type=F32)
    whole_high = whole.astype(BF16)
    wide_filter[:, :FLEN] = whole_high
    wide_filter[:, FLEN:] = (whole - whole_high.astype(F32)).astype(BF16)

    def filter_rows(rows):
        both = jnp.dot(halves(rows), wide_filter[...], preferred_element_type=F32)
        n = rows.shape[0]
        return both[:n, :FLEN] + both[n:, :FLEN] + both[:n, FLEN:]

    def project(z):
        z_high = z.astype(BF16).astype(F32)
        rows = []
        for part in (z_high, z - z_high):
            blocks = []
            for n in range(LISTED):
                s = n // KBLK
                blocks.append(jnp.where(row16 == n, part[:, s * SEGLEN : (s + 1) * SEGLEN], 0.0))
            rows.append(jnp.concatenate(blocks, axis=1))
        lhs = jnp.concatenate(rows, axis=0).astype(BF16)
        return folded(jnp.dot(lhs, pt[...], preferred_element_type=F32))

    arrived(x_copies)
    arrived(y_copies)
    y = ybuf[0]
    for d in range(1, n_det):
        y = y + ybuf[d]
    u = halves(jnp.broadcast_to(y[1:2, : n_det * MODES], (8, n_det * MODES)))
    squared_gain = y[1:2, FLEN - 1 : FLEN]

    def combine(total, group_rows):
        return total - folded(
            jnp.dot(u, group_rows[...].reshape(n_det * MODES, FLEN), preferred_element_type=F32)
        )

    r = combine(y[0:1], xbuf)
    pbuf[0] = project(filter_rows(r)[0:1]).astype(BF16)
    spread(pbuf, p_send, p_recv)

    for n in range(LISTED):
        pt_t[:, n * SEGLEN : (n + 1) * SEGLEN] = pt[n * SEGLEN : (n + 1) * SEGLEN, :].T
    gcol[...] = jnp.broadcast_to(g, (128, g.shape[1])).T
    vt_high = vt.astype(BF16).astype(F32)
    vt_low = vt - vt_high
    vcat[...] = jnp.concatenate([vt_high, vt_low, vt_high, jnp.zeros_like(vt)], axis=0).T.astype(BF16)
    arrived(l_copies)
    arrived(k_copies)
    k = kbuf[0]
    base_sum = xbuf[0].astype(F32)
    kept_sum = lbuf[0].astype(F32)
    for d in range(1, n_det):
        k = k + kbuf[d]
        base_sum = base_sum + xbuf[d].astype(F32)
        kept_sum = kept_sum + lbuf[d].astype(F32)
    k = combine(k, lbuf)
    all_of(wbuf, w_recv)
    info = wbuf[:, LISTED : 2 * LISTED, :].astype(F32)
    per = 128 // LISTED
    mine = iota((n_tm, LISTED, 128), 2) // LISTED == lax.rem(iota((n_tm, LISTED, 128), 0), per)
    info = jnp.sum(jnp.where(mine, info, 0.0).reshape(n_tm // per, per, LISTED, 128), axis=1)
    key = jnp.concatenate([info[c, 0:1] * 128.0 + info[c, 1:2] for c in range(n_tm // per)], axis=1)
    slot = det * n_tm + tm
    loads[9].wait()
    tile_mine = jnp.sum(
        jnp.where(owner[...] == slot, iota((1, 128), 1), 0).astype(F32), axis=1, keepdims=True
    )
    same = (own_key.astype(F32)[:, 0:1] == key).astype(F32).astype(BF16)
    into = (tile_mine * 128.0 + iota((128, listed), 0).astype(F32) == key).astype(F32).astype(BF16)
    all_squares = wbuf[:, :LISTED, :].reshape(listed, TILE)
    own_scale = 1.0 / (1.0 + squared_gain * jnp.dot(same, all_squares, preferred_element_type=F32))
    tile_weight = 1.0 + squared_gain * jnp.dot(into, all_squares, preferred_element_type=F32)
    tile_scale = jnp.sqrt(tile_weight) / tile_weight

    all_of(pbuf, p_recv)
    first = pbuf[...].reshape(listed, TILE)
    fetched = (jnp.dot(same, first, preferred_element_type=F32) * own_scale).astype(BF16)
    wide = jnp.dot(fetched, pt_t[...], preferred_element_type=F32)
    diagonal = iota((LISTED, LISTED * SEGLEN), 0) == iota((LISTED, LISTED * SEGLEN), 1) // SEGLEN
    flat = jnp.sum(jnp.where(diagonal, wide, 0.0), axis=0, keepdims=True)
    parts = []
    for s in range(SEG_DEV):
        total = flat[:, s * KBLK * SEGLEN : (s * KBLK + 1) * SEGLEN]
        for n in range(s * KBLK + 1, (s + 1) * KBLK):
            total = total + flat[:, n * SEGLEN : (n + 1) * SEGLEN]
        parts.append(total)
    sig = jnp.concatenate(parts, axis=1)
    qbuf[0] = project(filter_rows(r - sig * k)[0:1]).astype(BF16)
    spread(qbuf, q_send, q_recv)

    amp = filter_rows(base_sum - sig * kept_sum)
    amp_high = amp.astype(BF16).astype(F32)
    amp_cat = jnp.concatenate([amp_high, amp_high, amp - amp_high, jnp.zeros_like(amp)], axis=0).astype(BF16)
    chunk = 128

    def clean_rows(c, carry):
        at = pl.ds(pl.multiple_of(c * chunk, chunk), chunk)
        gains_here = jnp.concatenate([gcol[at, :]] * (FLEN // 128), axis=1)
        left = ((ts[at, :] - gains_here * sig) * keepb[at, :].astype(F32)).astype(BF16)
        shaped = (jnp.dot(left, table[...], preferred_element_type=F32) * response).astype(BF16)
        filtered = jnp.dot(shaped, table_t[...], preferred_element_type=F32)
        filtered = filtered - jnp.dot(vcat[at, :], amp_cat, preferred_element_type=F32)
        clean[at, :] = filtered.astype(BF16)
        return carry

    lax.fori_loop(0, ts.shape[0] // chunk, clean_rows, 0)
    sums = jnp.dot(into, first, preferred_element_type=F32)

    all_of(qbuf, q_recv)
    second = qbuf[...].reshape(listed, TILE)
    sums = sums + jnp.dot(into, second, preferred_element_type=F32)
    tile_out[...] = sums * tile_scale

    for copies in (x_copies, y_copies, l_copies, k_copies):
        for copy in copies:
            copy.wait_send()
    all_of(wbuf, w_send)
    all_of(pbuf, p_send)
    all_of(qbuf, q_send)


def solution(mesh):
    n_det, n_tm = mesh.shape["det"], mesh.shape["tm"]
    table_const = half_table()

    def shards(
        timestream, sample_flags, pointing, tile_ids, block_offsets, tile_owner, det_gains, mode_vectors, filter_gain
    ):
        dets, samples = timestream.shape
        hbm = pl.BlockSpec(memory_space=pltpu.HBM)
        vmem = pl.BlockSpec(memory_space=pltpu.VMEM)
        dma = pltpu.SemaphoreType.DMA
        tile_snr, cleaned = pl.pallas_call(
            functools.partial(kernel, n_det, n_tm),
            out_shape=(
                jax.ShapeDtypeStruct((TILE, TILE), F32),
                jax.ShapeDtypeStruct((dets, samples), BF16),
            ),
            in_specs=[hbm] * 10,
            out_specs=(vmem, vmem),
            scratch_shapes=[
                pltpu.VMEM((1, dets), F32),
                pltpu.VMEM((MODES, dets), F32),
                pltpu.VMEM((dets, samples), jnp.int32),
                pltpu.VMEM((dets, samples), F32),
                pltpu.VMEM((LISTED * SEGLEN, TILE), BF16),
                pltpu.SMEM((SEG_DEV, KBLK), jnp.int32),
                pltpu.SMEM((SEG_DEV, KBLK), jnp.int32),
                pltpu.VMEM((FLEN, FLEN), BF16),
                pltpu.VMEM((HALF + 1,), F32),
                pltpu.VMEM((1, tile_owner.shape[0]), jnp.int32),
                pltpu.VMEM((dets, samples), BF16),
                pltpu.VMEM((dets, 128), F32),
                pltpu.VMEM((dets, 128), BF16),
                pltpu.VMEM((FLEN, FLEN), BF16),
                pltpu.VMEM((TILE, LISTED * SEGLEN), BF16),
                pltpu.VMEM((FLEN, 2 * FLEN), BF16),
                pltpu.VMEM((n_det, 2, samples), F32),
                pltpu.VMEM((n_det, MODES, samples), BF16),
                pltpu.VMEM((n_det, MODES, samples), BF16),
                pltpu.VMEM((n_det, 1, samples), F32),
                pltpu.VMEM((n_tm, 2 * LISTED, TILE), BF16),
                pltpu.VMEM((n_tm, LISTED, TILE), BF16),
                pltpu.VMEM((n_tm, LISTED, TILE), BF16),
                pltpu.SemaphoreType.REGULAR,
                dma((10,)),
            ]
            + [dma((n_det - 1,))] * 8
            + [dma] * 6,
            compiler_params=pltpu.CompilerParams(
                collective_id=0, has_side_effects=True, vmem_limit_bytes=40 * 1024 * 1024
            ),
        )(
            *(
                pltpu.with_memory_space_constraint(operand, pltpu.HBM)
                for operand in (
                    det_gains.reshape(1, -1),
                    mode_vectors.T,
                    sample_flags,
                    timestream,
                    pointing.reshape(LISTED * SEGLEN, TILE),
                    tile_ids,
                    block_offsets,
                    jnp.asarray(table_const),
                    filter_gain,
                    tile_owner.reshape(1, -1),
                )
            )
        )
        return tile_snr.reshape(1, TILE, TILE), cleaned

    return jax.shard_map(
        shards,
        mesh=mesh,
        in_specs=(
            P("det", "tm"), P("det", "tm"), P("tm", None, None, None), P("tm", None), P("tm", None),
            P(), P("det"), P("det", None), P(),
        ),
        out_specs=(P(("det", "tm"), None, None), P("det", "tm")),
        check_vma=False,
    )
```

```python
import functools
import math

import jax
import jax.numpy as jnp
import ml_dtypes
import numpy as np
from jax import lax
from jax.experimental import pallas as pl
from jax.experimental.pallas import tpu as pltpu
from jax.sharding import PartitionSpec as P

FLEN = 512
HALF = FLEN // 2
TILE = 128
SEGLEN = 128
SEG_DEV = 4
KBLK = 4
LISTED = SEG_DEV * KBLK
MODES = 32
F32 = jnp.float32
BF16 = jnp.bfloat16
HI = lax.Precision.HIGHEST
MESH = pl.DeviceIdType.MESH
LAST = (((1,), (1,)), ((), ()))


def half_table():
    position = np.arange(FLEN)
    phase = position[:, None] * position[None, :] % FLEN
    angles = phase.astype(np.float32) * np.float32(2.0 * math.pi / FLEN)
    cosine, sine = np.cos(angles), np.sin(angles)
    table = np.concatenate([cosine[:, : HALF + 1], sine[:, 1:HALF]], axis=1)
    return table.astype(np.float32).astype(ml_dtypes.bfloat16)


def iota(shape, dim):
    return lax.broadcasted_iota(jnp.int32, shape, dim)


def halves(x):
    high = x.astype(BF16).astype(F32)
    return jnp.concatenate([high, x - high], axis=0).astype(BF16)


def folded(y):
    n = y.shape[0] // 2
    return y[:n] + y[n:]


def kernel(
    n_det, n_tm,
    gains_hbm, modes_hbm, fl_hbm, ts_hbm, pt_hbm, tids_hbm, offs_hbm, table_hbm, fgain_hbm, owner_hbm,
    tile_out, clean,
    gains, modes, fl, ts, pt, tids, offs, table, fgain, owner,
    keepb, gcol, vcat, table_t, pt_t, wide_filter,
    ybuf, xbuf, lbuf, kbuf, wbuf, idbuf, pbuf, qbuf,
    column_sem, core_sem, share_send, share_recv, in_sem, y_send, y_recv, x_send, x_recv, l_send, l_recv, k_send, k_recv,
    w_send, w_recv, id_send, id_recv, p_send, p_recv, q_send, q_recv,
):
    det, tm = lax.axis_index("det"), lax.axis_index("tm")
    listed = n_tm * LISTED

    loads = []
    pairs = (
        (gains_hbm, gains), (modes_hbm, modes), (fl_hbm, fl), (ts_hbm, ts), (pt_hbm, pt),
        (tids_hbm, tids), (offs_hbm, offs), (table_hbm, table), (fgain_hbm, fgain), (owner_hbm, owner),
    )
    for n, (src, dst) in enumerate(pairs):
        loads.append(pltpu.make_async_copy(src, dst, in_sem.at[n]))
        loads[-1].start()

    n_z = 4
    n_x = n_tm // (2 * n_z)
    half = n_tm // 2
    tm_x, tm_z, tm_core = tm // (2 * n_z), lax.rem(tm // 2, n_z), lax.rem(tm, 2)
    offsets = [(dx, dz, dc) for dx in range(n_x) for dz in range(n_z) for dc in range(2) if dx or dz or dc]
    offsets.sort(key=lambda o: -(min(o[0], n_x - o[0]) * 10 + min(o[1], n_z - o[1]) * 10 + o[2]))
    peers = []
    for dx, dz, dc in offsets:
        peer = (
            lax.rem(tm_x + dx, n_x) * (2 * n_z) + lax.rem(tm_z + dz, n_z) * 2 + lax.rem(tm_core + dc, 2)
        )
        peers.append((dc * half + dx * n_z + dz, {"tm": peer}))
    det_peers = [{"det": lax.rem(det + d, n_det)} for d in range(1, n_det)]

    barrier = pltpu.get_barrier_semaphore()
    row_peers = [peer for (_, dz, dc), (_, peer) in zip(offsets, peers) if dz == 0 and dc == 0]
    column_peers = [peer for (dx, _, dc), (_, peer) in zip(offsets, peers) if dx == 0 and dc == 0]
    plane_peers = [pair for (_, _, dc), pair in zip(offsets, peers) if dc == 0]
    sibling = {"tm": tm + 1 - 2 * tm_core}
    near = column_peers + det_peers + row_peers + [sibling]
    for peer in near:
        pl.semaphore_signal(barrier, inc=1, device_id=peer, device_id_type=MESH)

    def det_copies(buf, send, recv):
        return [
            pltpu.make_async_remote_copy(
                src_ref=buf.at[0], dst_ref=buf.at[d], send_sem=send.at[d - 1], recv_sem=recv.at[d - 1],
                device_id=det_peers[d - 1], device_id_type=MESH,
            )
            for d in range(1, n_det)
        ]

    def start(copies):
        for copy in copies:
            copy.start()

    def arrived(copies):
        for copy in copies:
            copy.wait_recv()

    def spread(buf, send, recv, to):
        for d, peer in to:
            pltpu.make_async_remote_copy(
                src_ref=buf.at[0], dst_ref=buf.at[d], send_sem=send, recv_sem=recv,
                device_id=peer, device_id_type=MESH,
            ).start()

    def all_of(buf, sem, count=n_tm - 1):
        rest = buf.at[pl.ds(1, count)]
        pltpu.make_async_copy(rest, rest, sem).wait()

    loads[0].wait()
    loads[1].wait()
    g = gains[...]
    vt = modes[...]
    copies_u = jnp.concatenate(
        [lax.dot_general(jnp.broadcast_to(g, (8, g.shape[1])), vt, LAST, precision=HI, preferred_element_type=F32)]
        * n_det,
        axis=1,
    )[0:1]
    squared = jnp.broadcast_to(jnp.sum(g * g, axis=1, keepdims=True), (1, FLEN - n_det * MODES))
    first8 = iota((8, FLEN), 0) == 0
    weights = jnp.concatenate([vt, jnp.where(first8, g, 0.0)], axis=0)
    weight_halves = halves(weights)

    loads[2].wait()
    loads[3].wait()
    keep = (1 - fl[...]).astype(F32)
    keepb[...] = keep.astype(BF16)
    residual = (ts[...] * keep).astype(BF16)
    base = folded(jnp.dot(weight_halves, residual, preferred_element_type=F32))
    xbuf[0] = base[:MODES].astype(BF16)
    ybuf[0] = jnp.concatenate([base[MODES : MODES + 1], jnp.concatenate([copies_u, squared], axis=1)], axis=0)
    pl.semaphore_wait(barrier, len(near))
    for peer in row_peers:
        pl.semaphore_signal(column_sem, inc=1, device_id=peer, device_id_type=MESH)
    x_copies = det_copies(xbuf, x_send, x_recv)
    y_copies = det_copies(ybuf, y_send, y_recv)
    start(x_copies)
    start(y_copies)

    for n in (4, 5, 6):
        loads[n].wait()
    pointing = pt[...].astype(F32)
    squares = jnp.sum((pointing * pointing).reshape(LISTED, SEGLEN, TILE), axis=1)
    lane16 = lax.rem(iota((1, 128), 1), LISTED)
    row16 = iota((LISTED, 128), 0)
    key_row = jnp.zeros((1, 128), jnp.int32)
    own_key = jnp.zeros((LISTED, 128), jnp.int32)
    for n in range(LISTED):
        own = tids[n // KBLK, n % KBLK] * 128 + offs[n // KBLK, n % KBLK]
        key_row = jnp.where(lane16 == n, own, key_row)
        own_key = jnp.where(row16 == n, own, own_key)
    wbuf[0] = squares.astype(BF16)
    idbuf[0] = key_row.astype(F32)
    pl.semaphore_wait(column_sem, len(row_peers))
    pl.semaphore_signal(core_sem, inc=1, device_id=sibling, device_id_type=MESH)
    spread(wbuf, w_send, w_recv, plane_peers)
    spread(idbuf, id_send, id_recv, plane_peers)

    kept = folded(jnp.dot(halves(weights * g), keepb[...], preferred_element_type=F32))
    lbuf[0] = kept[:MODES].astype(BF16)
    kbuf[0] = kept[MODES : MODES + 1]
    l_copies = det_copies(lbuf, l_send, l_recv)
    k_copies = det_copies(kbuf, k_send, k_recv)
    start(l_copies)
    start(k_copies)

    loads[8].wait()
    gain = fgain[...].reshape(1, HALF + 1)
    low = gain[:, :HALF]
    lane_half = iota((1, HALF), 1)
    response = jnp.concatenate(
        [
            jnp.where(lane_half == 0, low * (1.0 / FLEN), low * (2.0 / FLEN)),
            jnp.where(lane_half == 0, gain[:, HALF : HALF + 1] * (1.0 / FLEN), low * (2.0 / FLEN)),
        ],
        axis=1,
    )
    loads[7].wait()
    table_t[...] = table[...].T
    scaled = table[...].astype(F32) * response
    scaled_high = scaled.astype(BF16)
    scaled_low = (scaled - scaled_high.astype(F32)).astype(BF16)
    whole = jnp.dot(scaled_high, table_t[...], preferred_element_type=F32)
    whole = whole + jnp.dot(scaled_low, table_t[...], preferred_element_type=F32)
    whole_high = whole.astype(BF16)
    wide_filter[:, :FLEN] = whole_high
    wide_filter[:, FLEN:] = (whole - whole_high.astype(F32)).astype(BF16)

    def filter_rows(rows):
        both = jnp.dot(halves(rows), wide_filter[...], preferred_element_type=F32)
        n = rows.shape[0]
        return both[:n, :FLEN] + both[n:, :FLEN] + both[:n, FLEN:]

    def project(z):
        z_high = z.astype(BF16).astype(F32)
        rows = []
        for part in (z_high, z - z_high):
            blocks = []
            for n in range(LISTED):
                s = n // KBLK
                blocks.append(jnp.where(row16 == n, part[:, s * SEGLEN : (s + 1) * SEGLEN], 0.0))
            rows.append(jnp.concatenate(blocks, axis=1))
        lhs = jnp.concatenate(rows, axis=0).astype(BF16)
        return folded(jnp.dot(lhs, pt[...], preferred_element_type=F32))

    arrived(x_copies)
    arrived(y_copies)
    y = ybuf[0]
    for d in range(1, n_det):
        y = y + ybuf[d]
    u = halves(jnp.broadcast_to(y[1:2, : n_det * MODES], (8, n_det * MODES)))
    squared_gain = y[1:2, FLEN - 1 : FLEN]

    def combine(total, group_rows):
        return total - folded(
            jnp.dot(u, group_rows[...].reshape(n_det * MODES, FLEN), preferred_element_type=F32)
        )

    r = combine(y[0:1], xbuf)
    pbuf[0] = project(filter_rows(r)[0:1]).astype(BF16)
    pl.semaphore_wait(core_sem, 1)
    spread(pbuf, p_send, p_recv, peers)

    all_of(wbuf, w_recv, half - 1)
    all_of(idbuf, id_recv, half - 1)
    shares = [
        pltpu.make_async_remote_copy(
            src_ref=buf.at[pl.ds(0, half)], dst_ref=buf.at[pl.ds(half, half)],
            send_sem=share_send.at[n], recv_sem=share_recv.at[n], device_id=sibling, device_id_type=MESH,
        )
        for n, buf in enumerate((wbuf, idbuf))
    ]
    start(shares)
    for n in range(LISTED):
        pt_t[:, n * SEGLEN : (n + 1) * SEGLEN] = pt[n * SEGLEN : (n + 1) * SEGLEN, :].T
    gcol[...] = jnp.broadcast_to(g, (128, g.shape[1])).T
    vt_high = vt.astype(BF16).astype(F32)
    vt_low = vt - vt_high
    vcat[...] = jnp.concatenate([vt_high, vt_low, vt_high, jnp.zeros_like(vt)], axis=0).T.astype(BF16)
    arrived(l_copies)
    arrived(k_copies)
    k = kbuf[0]
    base_sum = xbuf[0].astype(F32)
    kept_sum = lbuf[0].astype(F32)
    for d in range(1, n_det):
        k = k + kbuf[d]
        base_sum = base_sum + xbuf[d].astype(F32)
        kept_sum = kept_sum + lbuf[d].astype(F32)
    k = combine(k, lbuf)
    arrived(shares)
    per = 128 // LISTED
    mine = iota((n_tm, 128), 1) // LISTED == lax.rem(iota((n_tm, 128), 0), per)
    spaced = jnp.where(mine, idbuf[...].reshape(n_tm, 128), 0.0).reshape(n_tm // per, per, 128)
    spaced = jnp.sum(spaced, axis=1, keepdims=True)
    key = jnp.concatenate([spaced[c] for c in range(n_tm // per)], axis=1)
    slot = det * n_tm + tm
    loads[9].wait()
    tile_mine = jnp.sum(
        jnp.where(owner[...] == slot, iota((1, 128), 1), 0).astype(F32), axis=1, keepdims=True
    )
    same = (own_key.astype(F32)[:, 0:1] == key).astype(F32).astype(BF16)
    into = (tile_mine * 128.0 + iota((128, listed), 0).astype(F32) == key).astype(F32).astype(BF16)
    all_squares = wbuf[...].reshape(listed, TILE)
    own_scale = 1.0 / (1.0 + squared_gain * jnp.dot(same, all_squares, preferred_element_type=F32))
    tile_weight = 1.0 + squared_gain * jnp.dot(into, all_squares, preferred_element_type=F32)
    tile_scale = jnp.sqrt(tile_weight) / tile_weight

    all_of(pbuf, p_recv)
    first = pbuf[...].reshape(listed, TILE)
    fetched = (jnp.dot(same, first, preferred_element_type=F32) * own_scale).astype(BF16)
    wide = jnp.dot(fetched, pt_t[...], preferred_element_type=F32)
    diagonal = iota((LISTED, LISTED * SEGLEN), 0) == iota((LISTED, LISTED * SEGLEN), 1) // SEGLEN
    flat = jnp.sum(jnp.where(diagonal, wide, 0.0), axis=0, keepdims=True)
    parts = []
    for s in range(SEG_DEV):
        total = flat[:, s * KBLK * SEGLEN : (s * KBLK + 1) * SEGLEN]
        for n in range(s * KBLK + 1, (s + 1) * KBLK):
            total = total + flat[:, n * SEGLEN : (n + 1) * SEGLEN]
        parts.append(total)
    sig = jnp.concatenate(parts, axis=1)
    qbuf[0] = project(filter_rows(r - sig * k)[0:1]).astype(BF16)
    spread(qbuf, q_send, q_recv, peers)

    amp = filter_rows(base_sum - sig * kept_sum)
    amp_high = amp.astype(BF16).astype(F32)
    amp_cat = jnp.concatenate([amp_high, amp_high, amp - amp_high, jnp.zeros_like(amp)], axis=0).astype(BF16)
    chunk = 128

    def clean_rows(c, carry):
        at = pl.ds(pl.multiple_of(c * chunk, chunk), chunk)
        gains_here = jnp.concatenate([gcol[at, :]] * (FLEN // 128), axis=1)
        left = ((ts[at, :] - gains_here * sig) * keepb[at, :].astype(F32)).astype(BF16)
        shaped = (jnp.dot(left, table[...], preferred_element_type=F32) * response).astype(BF16)
        filtered = jnp.dot(shaped, table_t[...], preferred_element_type=F32)
        filtered = filtered - jnp.dot(vcat[at, :], amp_cat, preferred_element_type=F32)
        clean[at, :] = filtered.astype(BF16)
        return carry

    lax.fori_loop(0, ts.shape[0] // chunk, clean_rows, 0)
    sums = jnp.dot(into, first, preferred_element_type=F32)

    all_of(qbuf, q_recv)
    second = qbuf[...].reshape(listed, TILE)
    sums = sums + jnp.dot(into, second, preferred_element_type=F32)
    tile_out[...] = sums * tile_scale

    for copies in (x_copies, y_copies, l_copies, k_copies, shares):
        for copy in copies:
            copy.wait_send()
    all_of(wbuf, w_send, half - 1)
    all_of(idbuf, id_send, half - 1)
    all_of(pbuf, p_send)
    all_of(qbuf, q_send)


def hand_out(tile, clean, tile_hbm, clean_hbm, sem):
    copies = [pltpu.make_async_copy(tile, tile_hbm, sem.at[0]), pltpu.make_async_copy(clean, clean_hbm, sem.at[1])]
    for copy in copies:
        copy.start()
    for copy in copies:
        copy.wait()


def solution(mesh):
    n_det, n_tm = mesh.shape["det"], mesh.shape["tm"]
    table_const = half_table()

    def shards(
        timestream, sample_flags, pointing, tile_ids, block_offsets, tile_owner, det_gains, mode_vectors, filter_gain
    ):
        dets, samples = timestream.shape
        hbm = pl.BlockSpec(memory_space=pltpu.HBM)
        vmem = pl.BlockSpec(memory_space=pltpu.VMEM)
        dma = pltpu.SemaphoreType.DMA
        tile_snr, cleaned = pl.pallas_call(
            functools.partial(kernel, n_det, n_tm),
            out_shape=(
                jax.ShapeDtypeStruct((TILE, TILE), F32),
                jax.ShapeDtypeStruct((dets, samples), BF16),
            ),
            in_specs=[hbm] * 10,
            out_specs=(vmem, vmem),
            scratch_shapes=[
                pltpu.VMEM((1, dets), F32),
                pltpu.VMEM((MODES, dets), F32),
                pltpu.VMEM((dets, samples), jnp.int32),
                pltpu.VMEM((dets, samples), F32),
                pltpu.VMEM((LISTED * SEGLEN, TILE), BF16),
                pltpu.SMEM((SEG_DEV, KBLK), jnp.int32),
                pltpu.SMEM((SEG_DEV, KBLK), jnp.int32),
                pltpu.VMEM((FLEN, FLEN), BF16),
                pltpu.VMEM((HALF + 1,), F32),
                pltpu.VMEM((1, tile_owner.shape[0]), jnp.int32),
                pltpu.VMEM((dets, samples), BF16),
                pltpu.VMEM((dets, 128), F32),
                pltpu.VMEM((dets, 128), BF16),
                pltpu.VMEM((FLEN, FLEN), BF16),
                pltpu.VMEM((TILE, LISTED * SEGLEN), BF16),
                pltpu.VMEM((FLEN, 2 * FLEN), BF16),
                pltpu.VMEM((n_det, 2, samples), F32),
                pltpu.VMEM((n_det, MODES, samples), BF16),
                pltpu.VMEM((n_det, MODES, samples), BF16),
                pltpu.VMEM((n_det, 1, samples), F32),
                pltpu.VMEM((n_tm, LISTED, TILE), BF16),
                pltpu.VMEM((n_tm, 1, 128), F32),
                pltpu.VMEM((n_tm, LISTED, TILE), BF16),
                pltpu.VMEM((n_tm, LISTED, TILE), BF16),
                pltpu.SemaphoreType.REGULAR,
                pltpu.SemaphoreType.REGULAR,
                dma((2,)),
                dma((2,)),
                dma((10,)),
            ]
            + [dma((n_det - 1,))] * 8
            + [dma] * 8,
            compiler_params=pltpu.CompilerParams(
                collective_id=0, has_side_effects=True, vmem_limit_bytes=40 * 1024 * 1024
            ),
        )(
            *(
                pltpu.with_memory_space_constraint(operand, pltpu.HBM)
                for operand in (
                    det_gains.reshape(1, -1),
                    mode_vectors.T,
                    sample_flags,
                    timestream,
                    pointing.reshape(LISTED * SEGLEN, TILE),
                    tile_ids,
                    block_offsets,
                    jnp.asarray(table_const),
                    filter_gain,
                    tile_owner.reshape(1, -1),
                )
            )
        )
        tile_snr, cleaned = pl.pallas_call(
            hand_out,
            out_shape=(
                jax.ShapeDtypeStruct((TILE, TILE), F32),
                jax.ShapeDtypeStruct((dets, samples), BF16),
            ),
            in_specs=[vmem, vmem],
            out_specs=(hbm, hbm),
            scratch_shapes=[dma((2,))],
        )(*(pltpu.with_memory_space_constraint(x, pltpu.VMEM) for x in (tile_snr, cleaned)))
        return tile_snr.reshape(1, TILE, TILE), cleaned

    return jax.shard_map(
        shards,
        mesh=mesh,
        in_specs=(
            P("det", "tm"), P("det", "tm"), P("tm", None, None, None), P("tm", None), P("tm", None),
            P(), P("det"), P("det", None), P(),
        ),
        out_specs=(P(("det", "tm"), None, None), P("det", "tm")),
        check_vma=False,
    )
```

```python
import functools
import math

import jax
import jax.numpy as jnp
import ml_dtypes
import numpy as np
from jax import lax
from jax.experimental import pallas as pl
from jax.experimental.pallas import tpu as pltpu
from jax.sharding import PartitionSpec as P

FLEN = 512
HALF = FLEN // 2
TILE = 128
SEGLEN = 128
SEG_DEV = 4
KBLK = 4
LISTED = SEG_DEV * KBLK
MODES = 32
F32 = jnp.float32
BF16 = jnp.bfloat16
HI = lax.Precision.HIGHEST
MESH = pl.DeviceIdType.MESH
LAST = (((1,), (1,)), ((), ()))


def half_table():
    position = np.arange(FLEN)
    phase = position[:, None] * position[None, :] % FLEN
    angles = phase.astype(np.float32) * np.float32(2.0 * math.pi / FLEN)
    cosine, sine = np.cos(angles), np.sin(angles)
    table = np.concatenate([cosine[:, : HALF + 1], sine[:, 1:HALF]], axis=1)
    return table.astype(np.float32).astype(ml_dtypes.bfloat16)


def iota(shape, dim):
    return lax.broadcasted_iota(jnp.int32, shape, dim)


def halves(x):
    high = x.astype(BF16).astype(F32)
    return jnp.concatenate([high, x - high], axis=0).astype(BF16)


def folded(y):
    n = y.shape[0] // 2
    return y[:n] + y[n:]


def kernel(
    n_det, n_tm,
    gains_hbm, modes_hbm, fl_hbm, ts_hbm, pt_hbm, tids_hbm, offs_hbm, table_hbm, fgain_hbm, owner_hbm,
    tile_out, clean,
    gains, modes, fl, ts, pt, tids, offs, table, fgain, owner,
    keepb, gcol, vcat, table_t, pt_t, wide_filter,
    ybuf, xbuf, lbuf, kbuf, wbuf, idbuf, pbuf, qbuf,
    column_sem, core_sem, share_send, share_recv, in_sem, y_send, y_recv, x_send, x_recv, l_send, l_recv, k_send, k_recv,
    w_send, w_recv, id_send, id_recv, p_send, p_recv, q_send, q_recv,
):
    det, tm = lax.axis_index("det"), lax.axis_index("tm")
    listed = n_tm * LISTED

    loads = []
    pairs = (
        (gains_hbm, gains), (modes_hbm, modes), (fl_hbm, fl), (ts_hbm, ts), (pt_hbm, pt),
        (tids_hbm, tids), (offs_hbm, offs), (table_hbm, table), (fgain_hbm, fgain), (owner_hbm, owner),
    )
    for n, (src, dst) in enumerate(pairs):
        loads.append(pltpu.make_async_copy(src, dst, in_sem.at[n]))
        loads[-1].start()

    n_z = 4
    n_x = n_tm // (2 * n_z)
    half = n_tm // 2
    tm_x, tm_z, tm_core = tm // (2 * n_z), lax.rem(tm // 2, n_z), lax.rem(tm, 2)
    offsets = [(dx, dz, dc) for dx in range(n_x) for dz in range(n_z) for dc in range(2) if dx or dz or dc]
    offsets.sort(key=lambda o: -(min(o[0], n_x - o[0]) * 10 + min(o[1], n_z - o[1]) * 10 + o[2]))
    peers = []
    for dx, dz, dc in offsets:
        peer = (
            lax.rem(tm_x + dx, n_x) * (2 * n_z) + lax.rem(tm_z + dz, n_z) * 2 + lax.rem(tm_core + dc, 2)
        )
        peers.append((dc * half + dx * n_z + dz, {"tm": peer}))
    det_peers = [{"det": lax.rem(det + d, n_det)} for d in range(1, n_det)]

    barrier = pltpu.get_barrier_semaphore()
    row_peers = [peer for (_, dz, dc), (_, peer) in zip(offsets, peers) if dz == 0 and dc == 0]
    column_peers = [peer for (dx, _, dc), (_, peer) in zip(offsets, peers) if dx == 0 and dc == 0]
    plane_peers = [pair for (_, _, dc), pair in zip(offsets, peers) if dc == 0]
    sibling = {"tm": tm + 1 - 2 * tm_core}
    near = column_peers + det_peers + row_peers + [sibling]
    for peer in near:
        pl.semaphore_signal(barrier, inc=1, device_id=peer, device_id_type=MESH)

    def spread_det(buf, send, recv):
        for d in (2, 1, 3):
            pltpu.make_async_remote_copy(
                src_ref=buf.at[0], dst_ref=buf.at[d], send_sem=send, recv_sem=recv,
                device_id=det_peers[d - 1], device_id_type=MESH,
            ).start()

    def spread(buf, send, recv, to):
        for d, peer in to:
            pltpu.make_async_remote_copy(
                src_ref=buf.at[0], dst_ref=buf.at[d], send_sem=send, recv_sem=recv,
                device_id=peer, device_id_type=MESH,
            ).start()

    def all_of(buf, sem, count):
        rest = buf.at[pl.ds(1, count)]
        pltpu.make_async_copy(rest, rest, sem).wait()

    loads[0].wait()
    loads[1].wait()
    g = gains[...]
    vt = modes[...]
    copies_u = jnp.concatenate(
        [lax.dot_general(jnp.broadcast_to(g, (8, g.shape[1])), vt, LAST, precision=HI, preferred_element_type=F32)]
        * n_det,
        axis=1,
    )[0:1]
    squared = jnp.broadcast_to(jnp.sum(g * g, axis=1, keepdims=True), (1, FLEN - n_det * MODES))
    first8 = iota((8, FLEN), 0) == 0
    weights = jnp.concatenate([vt, jnp.where(first8, g, 0.0)], axis=0)
    weight_halves = halves(weights)

    loads[2].wait()
    loads[3].wait()
    keep = (1 - fl[...]).astype(F32)
    keepb[...] = keep.astype(BF16)
    residual = (ts[...] * keep).astype(BF16)
    base = folded(jnp.dot(weight_halves, residual, preferred_element_type=F32))
    xbuf[0] = base[:MODES].astype(BF16)
    ybuf[0] = jnp.concatenate([base[MODES : MODES + 1], jnp.concatenate([copies_u, squared], axis=1)], axis=0)
    pl.semaphore_wait(barrier, len(near))
    for peer in row_peers:
        pl.semaphore_signal(column_sem, inc=1, device_id=peer, device_id_type=MESH)
    spread_det(xbuf, x_send, x_recv)
    spread_det(ybuf, y_send, y_recv)

    for n in (4, 5, 6):
        loads[n].wait()
    pointing = pt[...].astype(F32)
    squares = jnp.sum((pointing * pointing).reshape(LISTED, SEGLEN, TILE), axis=1)
    lane16 = lax.rem(iota((1, 128), 1), LISTED)
    row16 = iota((LISTED, 128), 0)
    key_row = jnp.zeros((1, 128), jnp.int32)
    own_key = jnp.zeros((LISTED, 128), jnp.int32)
    for n in range(LISTED):
        own = tids[n // KBLK, n % KBLK] * 128 + offs[n // KBLK, n % KBLK]
        key_row = jnp.where(lane16 == n, own, key_row)
        own_key = jnp.where(row16 == n, own, own_key)
    wbuf[0] = squares.astype(BF16)
    idbuf[0] = key_row.astype(F32)
    pl.semaphore_wait(column_sem, len(row_peers))
    pl.semaphore_signal(core_sem, inc=1, device_id=sibling, device_id_type=MESH)
    spread(wbuf, w_send, w_recv, plane_peers)
    spread(idbuf, id_send, id_recv, plane_peers)

    kept = folded(jnp.dot(halves(weights * g), keepb[...], preferred_element_type=F32))
    lbuf[0] = kept[:MODES].astype(BF16)
    kbuf[0] = kept[MODES : MODES + 1]
    spread_det(lbuf, l_send, l_recv)
    spread_det(kbuf, k_send, k_recv)

    loads[8].wait()
    gain = fgain[...].reshape(1, HALF + 1)
    low = gain[:, :HALF]
    lane_half = iota((1, HALF), 1)
    response = jnp.concatenate(
        [
            jnp.where(lane_half == 0, low * (1.0 / FLEN), low * (2.0 / FLEN)),
            jnp.where(lane_half == 0, gain[:, HALF : HALF + 1] * (1.0 / FLEN), low * (2.0 / FLEN)),
        ],
        axis=1,
    )
    loads[7].wait()
    table_t[...] = table[...].T
    scaled = table[...].astype(F32) * response
    scaled_high = scaled.astype(BF16)
    scaled_low = (scaled - scaled_high.astype(F32)).astype(BF16)
    whole = jnp.dot(scaled_high, table_t[...], preferred_element_type=F32)
    whole = whole + jnp.dot(scaled_low, table_t[...], preferred_element_type=F32)
    whole_high = whole.astype(BF16)
    wide_filter[:, :FLEN] = whole_high
    wide_filter[:, FLEN:] = (whole - whole_high.astype(F32)).astype(BF16)

    def filter_rows(rows):
        both = jnp.dot(halves(rows), wide_filter[...], preferred_element_type=F32)
        n = rows.shape[0]
        return both[:n, :FLEN] + both[n:, :FLEN] + both[:n, FLEN:]

    def project(z):
        z_high = z.astype(BF16).astype(F32)
        rows = []
        for part in (z_high, z - z_high):
            blocks = []
            for n in range(LISTED):
                s = n // KBLK
                blocks.append(jnp.where(row16 == n, part[:, s * SEGLEN : (s + 1) * SEGLEN], 0.0))
            rows.append(jnp.concatenate(blocks, axis=1))
        lhs = jnp.concatenate(rows, axis=0).astype(BF16)
        return folded(jnp.dot(lhs, pt[...], preferred_element_type=F32))

    all_of(xbuf, x_recv, n_det - 1)
    all_of(ybuf, y_recv, n_det - 1)
    y = ybuf[0]
    for d in range(1, n_det):
        y = y + ybuf[d]
    u = halves(jnp.broadcast_to(y[1:2, : n_det * MODES], (8, n_det * MODES)))
    squared_gain = y[1:2, FLEN - 1 : FLEN]

    def combine(total, group_rows):
        return total - folded(
            jnp.dot(u, group_rows[...].reshape(n_det * MODES, FLEN), preferred_element_type=F32)
        )

    r = combine(y[0:1], xbuf)
    pbuf[0] = project(filter_rows(r)[0:1]).astype(BF16)
    pl.semaphore_wait(core_sem, 1)
    spread(pbuf, p_send, p_recv, peers)

    all_of(wbuf, w_recv, half - 1)
    all_of(idbuf, id_recv, half - 1)
    shares = [
        pltpu.make_async_remote_copy(
            src_ref=buf.at[pl.ds(0, half)], dst_ref=buf.at[pl.ds(half, half)],
            send_sem=share_send.at[n], recv_sem=share_recv.at[n], device_id=sibling, device_id_type=MESH,
        )
        for n, buf in enumerate((wbuf, idbuf))
    ]
    for copy in shares:
        copy.start()
    for n in range(LISTED):
        pt_t[:, n * SEGLEN : (n + 1) * SEGLEN] = pt[n * SEGLEN : (n + 1) * SEGLEN, :].T
    gcol[...] = jnp.broadcast_to(g, (128, g.shape[1])).T
    vt_high = vt.astype(BF16).astype(F32)
    vt_low = vt - vt_high
    vcat[...] = jnp.concatenate([vt_high, vt_low, vt_high, jnp.zeros_like(vt)], axis=0).T.astype(BF16)
    all_of(lbuf, l_recv, n_det - 1)
    all_of(kbuf, k_recv, n_det - 1)
    k = kbuf[0]
    base_sum = xbuf[0].astype(F32)
    kept_sum = lbuf[0].astype(F32)
    for d in range(1, n_det):
        k = k + kbuf[d]
        base_sum = base_sum + xbuf[d].astype(F32)
        kept_sum = kept_sum + lbuf[d].astype(F32)
    k = combine(k, lbuf)
    for copy in shares:
        copy.wait_recv()
    per = 128 // LISTED
    mine = iota((n_tm, 128), 1) // LISTED == lax.rem(iota((n_tm, 128), 0), per)
    spaced = jnp.where(mine, idbuf[...].reshape(n_tm, 128), 0.0).reshape(n_tm // per, per, 128)
    spaced = jnp.sum(spaced, axis=1, keepdims=True)
    key = jnp.concatenate([spaced[c] for c in range(n_tm // per)], axis=1)
    slot = det * n_tm + tm
    loads[9].wait()
    tile_mine = jnp.sum(
        jnp.where(owner[...] == slot, iota((1, 128), 1), 0).astype(F32), axis=1, keepdims=True
    )
    same = (own_key.astype(F32)[:, 0:1] == key).astype(F32).astype(BF16)
    into = (tile_mine * 128.0 + iota((128, listed), 0).astype(F32) == key).astype(F32).astype(BF16)
    all_squares = wbuf[...].reshape(listed, TILE)
    own_scale = 1.0 / (1.0 + squared_gain * jnp.dot(same, all_squares, preferred_element_type=F32))
    tile_weight = 1.0 + squared_gain * jnp.dot(into, all_squares, preferred_element_type=F32)
    tile_scale = jnp.sqrt(tile_weight) / tile_weight

    all_of(pbuf, p_recv, n_tm - 1)
    first = pbuf[...].reshape(listed, TILE)
    fetched = (jnp.dot(same, first, preferred_element_type=F32) * own_scale).astype(BF16)
    wide = jnp.dot(fetched, pt_t[...], preferred_element_type=F32)
    diagonal = iota((LISTED, LISTED * SEGLEN), 0) == iota((LISTED, LISTED * SEGLEN), 1) // SEGLEN
    flat = jnp.sum(jnp.where(diagonal, wide, 0.0), axis=0, keepdims=True)
    parts = []
    for s in range(SEG_DEV):
        total = flat[:, s * KBLK * SEGLEN : (s * KBLK + 1) * SEGLEN]
        for n in range(s * KBLK + 1, (s + 1) * KBLK):
            total = total + flat[:, n * SEGLEN : (n + 1) * SEGLEN]
        parts.append(total)
    sig = jnp.concatenate(parts, axis=1)
    qbuf[0] = project(filter_rows(r - sig * k)[0:1]).astype(BF16)
    spread(qbuf, q_send, q_recv, peers)

    amp = filter_rows(base_sum - sig * kept_sum)
    amp_high = amp.astype(BF16).astype(F32)
    amp_cat = jnp.concatenate([amp_high, amp_high, amp - amp_high, jnp.zeros_like(amp)], axis=0).astype(BF16)
    chunk = 128

    def clean_rows(c, carry):
        at = pl.ds(pl.multiple_of(c * chunk, chunk), chunk)
        gains_here = jnp.concatenate([gcol[at, :]] * (FLEN // 128), axis=1)
        left = ((ts[at, :] - gains_here * sig) * keepb[at, :].astype(F32)).astype(BF16)
        shaped = (jnp.dot(left, table[...], preferred_element_type=F32) * response).astype(BF16)
        filtered = jnp.dot(shaped, table_t[...], preferred_element_type=F32)
        filtered = filtered - jnp.dot(vcat[at, :], amp_cat, preferred_element_type=F32)
        clean[at, :] = filtered.astype(BF16)
        return carry

    lax.fori_loop(0, ts.shape[0] // chunk, clean_rows, 0)
    sums = jnp.dot(into, first, preferred_element_type=F32)

    all_of(qbuf, q_recv, n_tm - 1)
    second = qbuf[...].reshape(listed, TILE)
    sums = sums + jnp.dot(into, second, preferred_element_type=F32)
    tile_out[...] = sums * tile_scale

    for buf, sem in ((xbuf, x_send), (ybuf, y_send), (lbuf, l_send), (kbuf, k_send)):
        all_of(buf, sem, n_det - 1)
    for copy in shares:
        copy.wait_send()
    all_of(wbuf, w_send, half - 1)
    all_of(idbuf, id_send, half - 1)
    all_of(pbuf, p_send, n_tm - 1)
    all_of(qbuf, q_send, n_tm - 1)


def hand_out(tile, clean, tile_hbm, clean_hbm, sem):
    copies = [pltpu.make_async_copy(tile, tile_hbm, sem.at[0]), pltpu.make_async_copy(clean, clean_hbm, sem.at[1])]
    for copy in copies:
        copy.start()
    for copy in copies:
        copy.wait()


def solution(mesh):
    n_det, n_tm = mesh.shape["det"], mesh.shape["tm"]
    table_const = half_table()

    def shards(
        timestream, sample_flags, pointing, tile_ids, block_offsets, tile_owner, det_gains, mode_vectors, filter_gain
    ):
        dets, samples = timestream.shape
        hbm = pl.BlockSpec(memory_space=pltpu.HBM)
        vmem = pl.BlockSpec(memory_space=pltpu.VMEM)
        dma = pltpu.SemaphoreType.DMA
        tile_snr, cleaned = pl.pallas_call(
            functools.partial(kernel, n_det, n_tm),
            out_shape=(
                jax.ShapeDtypeStruct((TILE, TILE), F32),
                jax.ShapeDtypeStruct((dets, samples), BF16),
            ),
            in_specs=[hbm] * 10,
            out_specs=(vmem, vmem),
            scratch_shapes=[
                pltpu.VMEM((1, dets), F32),
                pltpu.VMEM((MODES, dets), F32),
                pltpu.VMEM((dets, samples), jnp.int32),
                pltpu.VMEM((dets, samples), F32),
                pltpu.VMEM((LISTED * SEGLEN, TILE), BF16),
                pltpu.SMEM((SEG_DEV, KBLK), jnp.int32),
                pltpu.SMEM((SEG_DEV, KBLK), jnp.int32),
                pltpu.VMEM((FLEN, FLEN), BF16),
                pltpu.VMEM((HALF + 1,), F32),
                pltpu.VMEM((1, tile_owner.shape[0]), jnp.int32),
                pltpu.VMEM((dets, samples), BF16),
                pltpu.VMEM((dets, 128), F32),
                pltpu.VMEM((dets, 128), BF16),
                pltpu.VMEM((FLEN, FLEN), BF16),
                pltpu.VMEM((TILE, LISTED * SEGLEN), BF16),
                pltpu.VMEM((FLEN, 2 * FLEN), BF16),
                pltpu.VMEM((n_det, 2, samples), F32),
                pltpu.VMEM((n_det, MODES, samples), BF16),
                pltpu.VMEM((n_det, MODES, samples), BF16),
                pltpu.VMEM((n_det, 1, samples), F32),
                pltpu.VMEM((n_tm, LISTED, TILE), BF16),
                pltpu.VMEM((n_tm, 1, 128), F32),
                pltpu.VMEM((n_tm, LISTED, TILE), BF16),
                pltpu.VMEM((n_tm, LISTED, TILE), BF16),
                pltpu.SemaphoreType.REGULAR,
                pltpu.SemaphoreType.REGULAR,
                dma((2,)),
                dma((2,)),
                dma((10,)),
            ]
            + [dma] * 16,
            compiler_params=pltpu.CompilerParams(
                collective_id=0, has_side_effects=True, vmem_limit_bytes=40 * 1024 * 1024
            ),
        )(
            *(
                pltpu.with_memory_space_constraint(operand, pltpu.HBM)
                for operand in (
                    det_gains.reshape(1, -1),
                    mode_vectors.T,
                    sample_flags,
                    timestream,
                    pointing.reshape(LISTED * SEGLEN, TILE),
                    tile_ids,
                    block_offsets,
                    jnp.asarray(table_const),
                    filter_gain,
                    tile_owner.reshape(1, -1),
                )
            )
        )
        tile_snr, cleaned = pl.pallas_call(
            hand_out,
            out_shape=(
                jax.ShapeDtypeStruct((TILE, TILE), F32),
                jax.ShapeDtypeStruct((dets, samples), BF16),
            ),
            in_specs=[vmem, vmem],
            out_specs=(hbm, hbm),
            scratch_shapes=[dma((2,))],
        )(*(pltpu.with_memory_space_constraint(x, pltpu.VMEM) for x in (tile_snr, cleaned)))
        return tile_snr.reshape(1, TILE, TILE), cleaned

    return jax.shard_map(
        shards,
        mesh=mesh,
        in_specs=(
            P("det", "tm"), P("det", "tm"), P("tm", None, None, None), P("tm", None), P("tm", None),
            P(), P("det"), P("det", None), P(),
        ),
        out_specs=(P(("det", "tm"), None, None), P("det", "tm")),
        check_vma=False,
    )
```

```python
import functools
import math

import jax
import jax.numpy as jnp
import ml_dtypes
import numpy as np
from jax import lax
from jax.experimental import pallas as pl
from jax.experimental.pallas import tpu as pltpu
from jax.sharding import PartitionSpec as P

FLEN = 512
HALF = FLEN // 2
TILE = 128
SEGLEN = 128
SEG_DEV = 4
KBLK = 4
LISTED = SEG_DEV * KBLK
MODES = 32
F32 = jnp.float32
BF16 = jnp.bfloat16
HI = lax.Precision.HIGHEST
MESH = pl.DeviceIdType.MESH
LAST = (((1,), (1,)), ((), ()))


def half_table():
    position = np.arange(FLEN)
    phase = position[:, None] * position[None, :] % FLEN
    angles = phase.astype(np.float32) * np.float32(2.0 * math.pi / FLEN)
    cosine, sine = np.cos(angles), np.sin(angles)
    table = np.concatenate([cosine[:, : HALF + 1], sine[:, 1:HALF]], axis=1)
    return table.astype(np.float32).astype(ml_dtypes.bfloat16)


def iota(shape, dim):
    return lax.broadcasted_iota(jnp.int32, shape, dim)


def halves(x):
    high = x.astype(BF16).astype(F32)
    return jnp.concatenate([high, x - high], axis=0).astype(BF16)


def folded(y):
    n = y.shape[0] // 2
    return y[:n] + y[n:]


def kernel(
    n_det, n_tm,
    gains_hbm, modes_hbm, fl_hbm, ts_hbm, pt_hbm, tids_hbm, offs_hbm, table_hbm, fgain_hbm, owner_hbm,
    tile_out, clean,
    gains, modes, fl, ts, pt, tids, offs, table, fgain, owner,
    keepb, gcol, vcat, table_t, pt_t, wide_filter,
    ybuf, xbuf, lbuf, kbuf, wbuf, idbuf, pbuf, qbuf,
    column_sem, core_sem, share_send, share_recv, in_sem, y_send, y_recv, x_send, x_recv, l_send, l_recv, k_send, k_recv,
    w_send, w_recv, id_send, id_recv, p_send, p_recv, q_send, q_recv,
):
    det, tm = lax.axis_index("det"), lax.axis_index("tm")
    listed = n_tm * LISTED

    det_peers = [{"det": lax.rem(det + d, n_det)} for d in range(1, n_det)]
    barrier = pltpu.get_barrier_semaphore()
    for peer in det_peers:
        pl.semaphore_signal(barrier, inc=1, device_id=peer, device_id_type=MESH)

    loads = []
    pairs = (
        (gains_hbm, gains), (modes_hbm, modes), (fl_hbm, fl), (ts_hbm, ts), (pt_hbm, pt),
        (tids_hbm, tids), (offs_hbm, offs), (table_hbm, table), (fgain_hbm, fgain), (owner_hbm, owner),
    )
    for n, (src, dst) in enumerate(pairs):
        loads.append(pltpu.make_async_copy(src, dst, in_sem.at[n]))
        loads[-1].start()

    n_z = 4
    n_x = n_tm // (2 * n_z)
    half = n_tm // 2
    tm_x, tm_z, tm_core = tm // (2 * n_z), lax.rem(tm // 2, n_z), lax.rem(tm, 2)
    offsets = [(dx, dz, dc) for dx in range(n_x) for dz in range(n_z) for dc in range(2) if dx or dz or dc]
    offsets.sort(key=lambda o: -(min(o[0], n_x - o[0]) * 10 + min(o[1], n_z - o[1]) * 10 + o[2]))
    peers = []
    for dx, dz, dc in offsets:
        peer = (
            lax.rem(tm_x + dx, n_x) * (2 * n_z) + lax.rem(tm_z + dz, n_z) * 2 + lax.rem(tm_core + dc, 2)
        )
        peers.append((dc * half + dx * n_z + dz, {"tm": peer}))
    row_peers = [peer for (_, dz, dc), (_, peer) in zip(offsets, peers) if dz == 0 and dc == 0]
    column_peers = [peer for (dx, _, dc), (_, peer) in zip(offsets, peers) if dx == 0 and dc == 0]
    across = sorted(((dx, dc) for dx in range(n_x) for dc in range(2)), key=lambda o: -(min(o[0], n_x - o[0]) * 2 + o[1]))
    plane_peers = [pair for (_, _, dc), pair in zip(offsets, peers) if dc == 0]
    sibling = {"tm": tm + 1 - 2 * tm_core}
    near = column_peers + row_peers + [sibling]
    for peer in near:
        pl.semaphore_signal(barrier, inc=1, device_id=peer, device_id_type=MESH)

    def spread_det(buf, send, recv):
        for d in (2, 1, 3):
            pltpu.make_async_remote_copy(
                src_ref=buf.at[0], dst_ref=buf.at[d], send_sem=send, recv_sem=recv,
                device_id=det_peers[d - 1], device_id_type=MESH,
            ).start()

    def spread(buf, send, recv, to):
        for d, peer in to:
            pltpu.make_async_remote_copy(
                src_ref=buf.at[0], dst_ref=buf.at[d], send_sem=send, recv_sem=recv,
                device_id=peer, device_id_type=MESH,
            ).start()

    def spread_rows(buf, send, recv, targets):
        for z in targets:
            dz = lax.rem(z - tm_z + n_z, n_z)
            for dx, dc in across:
                slot = dc * half + dx * n_z + dz
                peer = (
                    lax.rem(tm_x + dx, n_x) * (2 * n_z) + z * 2 + lax.rem(tm_core + dc, 2)
                )

                def send_one(slot=slot, peer=peer):
                    pltpu.make_async_remote_copy(
                        src_ref=buf.at[0], dst_ref=buf.at[slot], send_sem=send, recv_sem=recv,
                        device_id={"tm": peer}, device_id_type=MESH,
                    ).start()

                if dx == 0 and dc == 0:
                    pl.when(dz != 0)(send_one)
                else:
                    send_one()

    def all_of(buf, sem, count):
        rest = buf.at[pl.ds(1, count)]
        pltpu.make_async_copy(rest, rest, sem).wait()

    loads[0].wait()
    loads[1].wait()
    g = gains[...]
    vt = modes[...]
    copies_u = jnp.concatenate(
        [lax.dot_general(jnp.broadcast_to(g, (8, g.shape[1])), vt, LAST, precision=HI, preferred_element_type=F32)]
        * n_det,
        axis=1,
    )[0:1]
    squared = jnp.broadcast_to(jnp.sum(g * g, axis=1, keepdims=True), (1, FLEN - n_det * MODES))
    first8 = iota((8, FLEN), 0) == 0
    weights = jnp.concatenate([vt, jnp.where(first8, g, 0.0)], axis=0)
    weight_halves = halves(weights)

    loads[2].wait()
    loads[3].wait()
    keep = (1 - fl[...]).astype(F32)
    keepb[...] = keep.astype(BF16)
    residual = (ts[...] * keep).astype(BF16)
    base = folded(jnp.dot(weight_halves, residual, preferred_element_type=F32))
    xbuf[0] = base[:MODES].astype(BF16)
    ybuf[0] = jnp.concatenate([base[MODES : MODES + 1], jnp.concatenate([copies_u, squared], axis=1)], axis=0)
    pl.semaphore_wait(barrier, len(det_peers) + len(near))
    spread_det(xbuf, x_send, x_recv)
    spread_det(ybuf, y_send, y_recv)
    for peer in row_peers:
        pl.semaphore_signal(column_sem, inc=1, device_id=peer, device_id_type=MESH)

    for n in (4, 5, 6):
        loads[n].wait()
    pointing = pt[...].astype(F32)
    squares = jnp.sum((pointing * pointing).reshape(LISTED, SEGLEN, TILE), axis=1)
    lane16 = lax.rem(iota((1, 128), 1), LISTED)
    row16 = iota((LISTED, 128), 0)
    key_row = jnp.zeros((1, 128), jnp.int32)
    own_key = jnp.zeros((LISTED, 128), jnp.int32)
    for n in range(LISTED):
        own = tids[n // KBLK, n % KBLK] * 128 + offs[n // KBLK, n % KBLK]
        key_row = jnp.where(lane16 == n, own, key_row)
        own_key = jnp.where(row16 == n, own, own_key)
    wbuf[0] = squares.astype(BF16)
    idbuf[0] = key_row.astype(F32)
    pl.semaphore_wait(column_sem, len(row_peers))
    pl.semaphore_signal(core_sem, inc=1, device_id=sibling, device_id_type=MESH)
    spread(wbuf, w_send, w_recv, plane_peers)
    spread(idbuf, id_send, id_recv, plane_peers)

    kept = folded(jnp.dot(halves(weights * g), keepb[...], preferred_element_type=F32))
    lbuf[0] = kept[:MODES].astype(BF16)
    kbuf[0] = kept[MODES : MODES + 1]
    spread_det(lbuf, l_send, l_recv)
    spread_det(kbuf, k_send, k_recv)

    loads[8].wait()
    gain = fgain[...].reshape(1, HALF + 1)
    low = gain[:, :HALF]
    lane_half = iota((1, HALF), 1)
    response = jnp.concatenate(
        [
            jnp.where(lane_half == 0, low * (1.0 / FLEN), low * (2.0 / FLEN)),
            jnp.where(lane_half == 0, gain[:, HALF : HALF + 1] * (1.0 / FLEN), low * (2.0 / FLEN)),
        ],
        axis=1,
    )
    loads[7].wait()
    table_t[...] = table[...].T
    scaled = table[...].astype(F32) * response
    scaled_high = scaled.astype(BF16)
    scaled_low = (scaled - scaled_high.astype(F32)).astype(BF16)
    whole = jnp.dot(scaled_high, table_t[...], preferred_element_type=F32)
    whole = whole + jnp.dot(scaled_low, table_t[...], preferred_element_type=F32)
    whole_high = whole.astype(BF16)
    wide_filter[:, :FLEN] = whole_high
    wide_filter[:, FLEN:] = (whole - whole_high.astype(F32)).astype(BF16)

    def filter_rows(rows):
        both = jnp.dot(halves(rows), wide_filter[...], preferred_element_type=F32)
        n = rows.shape[0]
        return both[:n, :FLEN] + both[n:, :FLEN] + both[:n, FLEN:]

    def project(z):
        z_high = z.astype(BF16).astype(F32)
        blocks = []
        for n in range(LISTED):
            s = n // KBLK
            blocks.append(jnp.where(row16 == n, z_high[:, s * SEGLEN : (s + 1) * SEGLEN], 0.0))
        lhs = jnp.concatenate(blocks, axis=1).astype(BF16)
        return jnp.dot(lhs, pt[...], preferred_element_type=F32)

    all_of(xbuf, x_recv, n_det - 1)
    all_of(ybuf, y_recv, n_det - 1)
    y = ybuf[0]
    for d in range(1, n_det):
        y = y + ybuf[d]
    u = halves(jnp.broadcast_to(y[1:2, : n_det * MODES], (8, n_det * MODES)))
    squared_gain = y[1:2, FLEN - 1 : FLEN]

    def combine(total, group_rows):
        return total - folded(
            jnp.dot(u, group_rows[...].reshape(n_det * MODES, FLEN), preferred_element_type=F32)
        )

    r = combine(y[0:1], xbuf)
    pbuf[0] = project(filter_rows(r)[0:1]).astype(BF16)
    pl.semaphore_wait(core_sem, 1)
    spread_rows(pbuf, p_send, p_recv, (2, 1, 3, 0))

    all_of(wbuf, w_recv, half - 1)
    all_of(idbuf, id_recv, half - 1)
    shares = [
        pltpu.make_async_remote_copy(
            src_ref=buf.at[pl.ds(0, half)], dst_ref=buf.at[pl.ds(half, half)],
            send_sem=share_send.at[n], recv_sem=share_recv.at[n], device_id=sibling, device_id_type=MESH,
        )
        for n, buf in enumerate((wbuf, idbuf))
    ]
    for copy in shares:
        copy.start()
    for n in range(LISTED):
        pt_t[:, n * SEGLEN : (n + 1) * SEGLEN] = pt[n * SEGLEN : (n + 1) * SEGLEN, :].T
    gcol[...] = jnp.broadcast_to(g, (128, g.shape[1])).T
    vt_high = vt.astype(BF16).astype(F32)
    vt_low = vt - vt_high
    vcat[...] = jnp.concatenate([vt_high, vt_low, vt_high, jnp.zeros_like(vt)], axis=0).T.astype(BF16)
    all_of(lbuf, l_recv, n_det - 1)
    all_of(kbuf, k_recv, n_det - 1)
    k = kbuf[0]
    base_sum = xbuf[0].astype(F32)
    kept_sum = lbuf[0].astype(F32)
    for d in range(1, n_det):
        k = k + kbuf[d]
        base_sum = base_sum + xbuf[d].astype(F32)
        kept_sum = kept_sum + lbuf[d].astype(F32)
    k = combine(k, lbuf)
    for copy in shares:
        copy.wait_recv()
    per = 128 // LISTED
    mine = iota((n_tm, 128), 1) // LISTED == lax.rem(iota((n_tm, 128), 0), per)
    spaced = jnp.where(mine, idbuf[...].reshape(n_tm, 128), 0.0).reshape(n_tm // per, per, 128)
    spaced = jnp.sum(spaced, axis=1, keepdims=True)
    key = jnp.concatenate([spaced[c] for c in range(n_tm // per)], axis=1)
    slot = det * n_tm + tm
    loads[9].wait()
    tile_mine = jnp.sum(
        jnp.where(owner[...] == slot, iota((1, 128), 1), 0).astype(F32), axis=1, keepdims=True
    )
    same = (own_key.astype(F32)[:, 0:1] == key).astype(F32).astype(BF16)
    into = (tile_mine * 128.0 + iota((128, listed), 0).astype(F32) == key).astype(F32).astype(BF16)
    all_squares = wbuf[...].reshape(listed, TILE)
    own_scale = 1.0 / (1.0 + squared_gain * jnp.dot(same, all_squares, preferred_element_type=F32))
    tile_weight = 1.0 + squared_gain * jnp.dot(into, all_squares, preferred_element_type=F32)
    tile_scale = jnp.sqrt(tile_weight) / tile_weight

    all_of(pbuf, p_recv, n_tm - 1)
    first = pbuf[...].reshape(listed, TILE)
    fetched = (jnp.dot(same, first, preferred_element_type=F32) * own_scale).astype(BF16)
    wide = jnp.dot(fetched, pt_t[...], preferred_element_type=F32)
    diagonal = iota((LISTED, LISTED * SEGLEN), 0) == iota((LISTED, LISTED * SEGLEN), 1) // SEGLEN
    flat = jnp.sum(jnp.where(diagonal, wide, 0.0), axis=0, keepdims=True)
    parts = []
    for s in range(SEG_DEV):
        total = flat[:, s * KBLK * SEGLEN : (s * KBLK + 1) * SEGLEN]
        for n in range(s * KBLK + 1, (s + 1) * KBLK):
            total = total + flat[:, n * SEGLEN : (n + 1) * SEGLEN]
        parts.append(total)
    sig = jnp.concatenate(parts, axis=1)
    qbuf[0] = project(filter_rows(r - sig * k)[0:1]).astype(BF16)
    spread_rows(qbuf, q_send, q_recv, (0, 1, 3, 2))

    amp = filter_rows(base_sum - sig * kept_sum)
    amp_high = amp.astype(BF16).astype(F32)
    amp_cat = jnp.concatenate([amp_high, amp_high, amp - amp_high, jnp.zeros_like(amp)], axis=0).astype(BF16)
    chunk = 128

    def clean_rows(c, carry):
        at = pl.ds(pl.multiple_of(c * chunk, chunk), chunk)
        gains_here = jnp.concatenate([gcol[at, :]] * (FLEN // 128), axis=1)
        left = ((ts[at, :] - gains_here * sig) * keepb[at, :].astype(F32)).astype(BF16)
        shaped = (jnp.dot(left, table[...], preferred_element_type=F32) * response).astype(BF16)
        filtered = jnp.dot(shaped, table_t[...], preferred_element_type=F32)
        filtered = filtered - jnp.dot(vcat[at, :], amp_cat, preferred_element_type=F32)
        clean[at, :] = filtered.astype(BF16)
        return carry

    lax.fori_loop(0, ts.shape[0] // chunk, clean_rows, 0)
    sums = jnp.dot(into, first, preferred_element_type=F32)

    all_of(qbuf, q_recv, n_tm - 1)
    second = qbuf[...].reshape(listed, TILE)
    sums = sums + jnp.dot(into, second, preferred_element_type=F32)
    tile_out[...] = sums * tile_scale

    for buf, sem in ((xbuf, x_send), (ybuf, y_send), (lbuf, l_send), (kbuf, k_send)):
        all_of(buf, sem, n_det - 1)
    for copy in shares:
        copy.wait_send()
    all_of(wbuf, w_send, half - 1)
    all_of(idbuf, id_send, half - 1)
    all_of(pbuf, p_send, n_tm - 1)
    all_of(qbuf, q_send, n_tm - 1)


def hand_out(tile, clean, tile_hbm, clean_hbm, sem):
    copies = [pltpu.make_async_copy(tile, tile_hbm, sem.at[0]), pltpu.make_async_copy(clean, clean_hbm, sem.at[1])]
    for copy in copies:
        copy.start()
    for copy in copies:
        copy.wait()


def solution(mesh):
    n_det, n_tm = mesh.shape["det"], mesh.shape["tm"]
    table_const = half_table()

    def shards(
        timestream, sample_flags, pointing, tile_ids, block_offsets, tile_owner, det_gains, mode_vectors, filter_gain
    ):
        dets, samples = timestream.shape
        hbm = pl.BlockSpec(memory_space=pltpu.HBM)
        vmem = pl.BlockSpec(memory_space=pltpu.VMEM)
        dma = pltpu.SemaphoreType.DMA
        tile_snr, cleaned = pl.pallas_call(
            functools.partial(kernel, n_det, n_tm),
            out_shape=(
                jax.ShapeDtypeStruct((TILE, TILE), F32),
                jax.ShapeDtypeStruct((dets, samples), BF16),
            ),
            in_specs=[hbm] * 10,
            out_specs=(vmem, vmem),
            scratch_shapes=[
                pltpu.VMEM((1, dets), F32),
                pltpu.VMEM((MODES, dets), F32),
                pltpu.VMEM((dets, samples), jnp.int32),
                pltpu.VMEM((dets, samples), F32),
                pltpu.VMEM((LISTED * SEGLEN, TILE), BF16),
                pltpu.SMEM((SEG_DEV, KBLK), jnp.int32),
                pltpu.SMEM((SEG_DEV, KBLK), jnp.int32),
                pltpu.VMEM((FLEN, FLEN), BF16),
                pltpu.VMEM((HALF + 1,), F32),
                pltpu.VMEM((1, tile_owner.shape[0]), jnp.int32),
                pltpu.VMEM((dets, samples), BF16),
                pltpu.VMEM((dets, 128), F32),
                pltpu.VMEM((dets, 128), BF16),
                pltpu.VMEM((FLEN, FLEN), BF16),
                pltpu.VMEM((TILE, LISTED * SEGLEN), BF16),
                pltpu.VMEM((FLEN, 2 * FLEN), BF16),
                pltpu.VMEM((n_det, 2, samples), F32),
                pltpu.VMEM((n_det, MODES, samples), BF16),
                pltpu.VMEM((n_det, MODES, samples), BF16),
                pltpu.VMEM((n_det, 1, samples), F32),
                pltpu.VMEM((n_tm, LISTED, TILE), BF16),
                pltpu.VMEM((n_tm, 1, 128), F32),
                pltpu.VMEM((n_tm, LISTED, TILE), BF16),
                pltpu.VMEM((n_tm, LISTED, TILE), BF16),
                pltpu.SemaphoreType.REGULAR,
                pltpu.SemaphoreType.REGULAR,
                dma((2,)),
                dma((2,)),
                dma((10,)),
            ]
            + [dma] * 16,
            compiler_params=pltpu.CompilerParams(
                collective_id=0, has_side_effects=True, vmem_limit_bytes=40 * 1024 * 1024
            ),
        )(
            *(
                pltpu.with_memory_space_constraint(operand, pltpu.HBM)
                for operand in (
                    det_gains.reshape(1, -1),
                    mode_vectors.T,
                    sample_flags,
                    timestream,
                    pointing.reshape(LISTED * SEGLEN, TILE),
                    tile_ids,
                    block_offsets,
                    jnp.asarray(table_const),
                    filter_gain,
                    tile_owner.reshape(1, -1),
                )
            )
        )
        tile_snr, cleaned = pl.pallas_call(
            hand_out,
            out_shape=(
                jax.ShapeDtypeStruct((TILE, TILE), F32),
                jax.ShapeDtypeStruct((dets, samples), BF16),
            ),
            in_specs=[vmem, vmem],
            out_specs=(hbm, hbm),
            scratch_shapes=[dma((2,))],
        )(*(pltpu.with_memory_space_constraint(x, pltpu.VMEM) for x in (tile_snr, cleaned)))
        return tile_snr.reshape(1, TILE, TILE), cleaned

    return jax.shard_map(
        shards,
        mesh=mesh,
        in_specs=(
            P("det", "tm"), P("det", "tm"), P("tm", None, None, None), P("tm", None), P("tm", None),
            P(), P("det"), P("det", None), P(),
        ),
        out_specs=(P(("det", "tm"), None, None), P("det", "tm")),
        check_vma=False,
    )
```

```python
import functools
import math

import jax
import jax.numpy as jnp
import ml_dtypes
import numpy as np
from jax import lax
from jax.experimental import pallas as pl
from jax.experimental.pallas import tpu as pltpu
from jax.sharding import PartitionSpec as P

FLEN = 512
HALF = FLEN // 2
TILE = 128
SEGLEN = 128
SEG_DEV = 4
KBLK = 4
LISTED = SEG_DEV * KBLK
MODES = 32
F32 = jnp.float32
BF16 = jnp.bfloat16
HI = lax.Precision.HIGHEST
MESH = pl.DeviceIdType.MESH
LAST = (((1,), (1,)), ((), ()))


def half_table():
    position = np.arange(FLEN)
    phase = position[:, None] * position[None, :] % FLEN
    angles = phase.astype(np.float32) * np.float32(2.0 * math.pi / FLEN)
    cosine, sine = np.cos(angles), np.sin(angles)
    table = np.concatenate([cosine[:, : HALF + 1], sine[:, 1:HALF]], axis=1)
    return table.astype(np.float32).astype(ml_dtypes.bfloat16)


def iota(shape, dim):
    return lax.broadcasted_iota(jnp.int32, shape, dim)


def halves(x):
    high = x.astype(BF16).astype(F32)
    return jnp.concatenate([high, x - high], axis=0).astype(BF16)


def folded(y):
    n = y.shape[0] // 2
    return y[:n] + y[n:]


def kernel(
    n_det, n_tm,
    gains_hbm, modes_hbm, fl_hbm, ts_hbm, pt_hbm, tids_hbm, offs_hbm, table_hbm, fgain_hbm, owner_hbm,
    tile_out, clean,
    gains, modes, fl, ts, pt, tids, offs, table, fgain, owner,
    keepb, gcol, vcat, table_t, pt_t, wide_filter,
    ybuf, xbuf, lbuf, kbuf, wbuf, idbuf, pbuf, qbuf,
    column_sem, core_sem, share_send, share_recv, in_sem, y_send, y_recv, x_send, x_recv, l_send, l_recv, k_send, k_recv,
    w_send, w_recv, id_send, id_recv, p_send, p_recv, q_send, q_recv,
):
    det, tm = lax.axis_index("det"), lax.axis_index("tm")
    listed = n_tm * LISTED

    det_peers = [{"det": lax.rem(det + d, n_det)} for d in range(1, n_det)]
    barrier = pltpu.get_barrier_semaphore()
    for peer in det_peers:
        pl.semaphore_signal(barrier, inc=1, device_id=peer, device_id_type=MESH)

    loads = []
    pairs = (
        (gains_hbm, gains), (modes_hbm, modes), (fl_hbm, fl), (ts_hbm, ts), (pt_hbm, pt),
        (tids_hbm, tids), (offs_hbm, offs), (table_hbm, table), (fgain_hbm, fgain), (owner_hbm, owner),
    )
    for n, (src, dst) in enumerate(pairs):
        loads.append(pltpu.make_async_copy(src, dst, in_sem.at[n]))
        loads[-1].start()

    n_z = 4
    n_x = n_tm // (2 * n_z)
    half = n_tm // 2
    tm_x, tm_z, tm_core = tm // (2 * n_z), lax.rem(tm // 2, n_z), lax.rem(tm, 2)
    offsets = [(dx, dz, dc) for dx in range(n_x) for dz in range(n_z) for dc in range(2) if dx or dz or dc]
    offsets.sort(key=lambda o: -(min(o[0], n_x - o[0]) * 10 + min(o[1], n_z - o[1]) * 10 + o[2]))
    peers = []
    for dx, dz, dc in offsets:
        peer = (
            lax.rem(tm_x + dx, n_x) * (2 * n_z) + lax.rem(tm_z + dz, n_z) * 2 + lax.rem(tm_core + dc, 2)
        )
        peers.append((dc * half + dx * n_z + dz, {"tm": peer}))
    row_peers = [peer for (_, dz, dc), (_, peer) in zip(offsets, peers) if dz == 0 and dc == 0]
    column_peers = [peer for (dx, _, dc), (_, peer) in zip(offsets, peers) if dx == 0 and dc == 0]
    across = sorted(((dx, dc) for dx in range(n_x) for dc in range(2)), key=lambda o: -(min(o[0], n_x - o[0]) * 2 + o[1]))
    plane_peers = [pair for (_, _, dc), pair in zip(offsets, peers) if dc == 0]
    sibling = {"tm": tm + 1 - 2 * tm_core}
    near = column_peers + row_peers + [sibling]
    for peer in near:
        pl.semaphore_signal(barrier, inc=1, device_id=peer, device_id_type=MESH)

    def spread_det(buf, send, recv):
        for d in (2, 1, 3):
            pltpu.make_async_remote_copy(
                src_ref=buf.at[0], dst_ref=buf.at[d], send_sem=send, recv_sem=recv,
                device_id=det_peers[d - 1], device_id_type=MESH,
            ).start()

    def spread(buf, send, recv, to):
        for d, peer in to:
            pltpu.make_async_remote_copy(
                src_ref=buf.at[0], dst_ref=buf.at[d], send_sem=send, recv_sem=recv,
                device_id=peer, device_id_type=MESH,
            ).start()

    def spread_rows(buf, send, recv, targets):
        for z in targets:
            dz = lax.rem(z - tm_z + n_z, n_z)
            for dx, dc in across:
                slot = dc * half + dx * n_z + dz
                peer = (
                    lax.rem(tm_x + dx, n_x) * (2 * n_z) + z * 2 + lax.rem(tm_core + dc, 2)
                )

                def send_one(slot=slot, peer=peer):
                    pltpu.make_async_remote_copy(
                        src_ref=buf.at[0], dst_ref=buf.at[slot], send_sem=send, recv_sem=recv,
                        device_id={"tm": peer}, device_id_type=MESH,
                    ).start()

                if dx == 0 and dc == 0:
                    pl.when(dz != 0)(send_one)
                else:
                    send_one()

    def all_of(buf, sem, count):
        rest = buf.at[pl.ds(1, count)]
        pltpu.make_async_copy(rest, rest, sem).wait()

    loads[0].wait()
    loads[1].wait()
    g = gains[...]
    vt = modes[...]
    copies_u = jnp.concatenate(
        [lax.dot_general(jnp.broadcast_to(g, (8, g.shape[1])), vt, LAST, precision=HI, preferred_element_type=F32)]
        * n_det,
        axis=1,
    )[0:1]
    squared = jnp.broadcast_to(jnp.sum(g * g, axis=1, keepdims=True), (1, FLEN - n_det * MODES))
    first8 = iota((8, FLEN), 0) == 0
    weights = jnp.concatenate([vt, jnp.where(first8, g, 0.0)], axis=0)
    weight_halves = halves(weights)

    loads[2].wait()
    loads[3].wait()
    keep = (1 - fl[...]).astype(F32)
    keepb[...] = keep.astype(BF16)
    residual = (ts[...] * keep).astype(BF16)
    base = folded(jnp.dot(weight_halves, residual, preferred_element_type=F32))
    xbuf[0] = base[:MODES].astype(BF16)
    ybuf[0] = jnp.concatenate([base[MODES : MODES + 1], jnp.concatenate([copies_u, squared], axis=1)], axis=0)
    pl.semaphore_wait(barrier, len(det_peers) + len(near))
    spread_det(xbuf, x_send, x_recv)
    spread_det(ybuf, y_send, y_recv)
    for peer in row_peers:
        pl.semaphore_signal(column_sem, inc=1, device_id=peer, device_id_type=MESH)

    for n in (4, 5, 6):
        loads[n].wait()
    pointing = pt[...].astype(F32)
    squares = jnp.sum((pointing * pointing).reshape(LISTED, SEGLEN, TILE), axis=1)
    lane16 = lax.rem(iota((1, 128), 1), LISTED)
    row16 = iota((LISTED, 128), 0)
    key_row = jnp.zeros((1, 128), jnp.int32)
    own_key = jnp.zeros((LISTED, 128), jnp.int32)
    for n in range(LISTED):
        own = tids[n // KBLK, n % KBLK] * 128 + offs[n // KBLK, n % KBLK]
        key_row = jnp.where(lane16 == n, own, key_row)
        own_key = jnp.where(row16 == n, own, own_key)
    wbuf[0] = squares.astype(BF16)
    idbuf[0] = key_row.astype(F32)
    pl.semaphore_wait(column_sem, len(row_peers))
    pl.semaphore_signal(core_sem, inc=1, device_id=sibling, device_id_type=MESH)
    spread(wbuf, w_send, w_recv, plane_peers)
    spread(idbuf, id_send, id_recv, plane_peers)

    kept = folded(jnp.dot(halves(weights * g), keepb[...], preferred_element_type=F32))
    lbuf[0] = kept[:MODES].astype(BF16)
    kbuf[0] = kept[MODES : MODES + 1]
    spread_det(lbuf, l_send, l_recv)
    spread_det(kbuf, k_send, k_recv)

    loads[8].wait()
    gain = fgain[...].reshape(1, HALF + 1)
    low = gain[:, :HALF]
    lane_half = iota((1, HALF), 1)
    response = jnp.concatenate(
        [
            jnp.where(lane_half == 0, low * (1.0 / FLEN), low * (2.0 / FLEN)),
            jnp.where(lane_half == 0, gain[:, HALF : HALF + 1] * (1.0 / FLEN), low * (2.0 / FLEN)),
        ],
        axis=1,
    )
    loads[7].wait()
    table_t[...] = table[...].T
    scaled = table[...].astype(F32) * response
    scaled_high = scaled.astype(BF16)
    scaled_low = (scaled - scaled_high.astype(F32)).astype(BF16)
    whole = jnp.dot(scaled_high, table_t[...], preferred_element_type=F32)
    whole = whole + jnp.dot(scaled_low, table_t[...], preferred_element_type=F32)
    whole_high = whole.astype(BF16)
    wide_filter[:, :FLEN] = whole_high
    wide_filter[:, FLEN:] = (whole - whole_high.astype(F32)).astype(BF16)

    def filter_rows(rows):
        both = jnp.dot(halves(rows), wide_filter[...], preferred_element_type=F32)
        n = rows.shape[0]
        return both[:n, :FLEN] + both[n:, :FLEN] + both[:n, FLEN:]

    def project(z):
        z_high = z.astype(BF16).astype(F32)
        rows = []
        for part in (z_high, z - z_high):
            blocks = []
            for n in range(LISTED):
                s = n // KBLK
                blocks.append(jnp.where(row16 == n, part[:, s * SEGLEN : (s + 1) * SEGLEN], 0.0))
            rows.append(jnp.concatenate(blocks, axis=1))
        lhs = jnp.concatenate(rows, axis=0).astype(BF16)
        return folded(jnp.dot(lhs, pt[...], preferred_element_type=F32))

    all_of(xbuf, x_recv, n_det - 1)
    all_of(ybuf, y_recv, n_det - 1)
    y = ybuf[0]
    for d in range(1, n_det):
        y = y + ybuf[d]
    u = halves(jnp.broadcast_to(y[1:2, : n_det * MODES], (8, n_det * MODES)))
    squared_gain = y[1:2, FLEN - 1 : FLEN]

    def combine(total, group_rows):
        return total - folded(
            jnp.dot(u, group_rows[...].reshape(n_det * MODES, FLEN), preferred_element_type=F32)
        )

    r = combine(y[0:1], xbuf)
    pbuf[0] = project(filter_rows(r)[0:1]).astype(BF16)
    pl.semaphore_wait(core_sem, 1)
    spread_rows(pbuf, p_send, p_recv, (2, 1, 3, 0))

    all_of(wbuf, w_recv, half - 1)
    all_of(idbuf, id_recv, half - 1)
    shares = [
        pltpu.make_async_remote_copy(
            src_ref=buf.at[pl.ds(0, half)], dst_ref=buf.at[pl.ds(half, half)],
            send_sem=share_send.at[n], recv_sem=share_recv.at[n], device_id=sibling, device_id_type=MESH,
        )
        for n, buf in enumerate((wbuf, idbuf))
    ]
    for copy in shares:
        copy.start()
    for n in range(LISTED):
        pt_t[:, n * SEGLEN : (n + 1) * SEGLEN] = pt[n * SEGLEN : (n + 1) * SEGLEN, :].T
    gcol[...] = jnp.broadcast_to(g, (128, g.shape[1])).T
    vt_high = vt.astype(BF16).astype(F32)
    vt_low = vt - vt_high
    vcat[...] = jnp.concatenate([vt_high, vt_low, vt_high, jnp.zeros_like(vt)], axis=0).T.astype(BF16)
    all_of(lbuf, l_recv, n_det - 1)
    all_of(kbuf, k_recv, n_det - 1)
    k = kbuf[0]
    base_sum = xbuf[0].astype(F32)
    kept_sum = lbuf[0].astype(F32)
    for d in range(1, n_det):
        k = k + kbuf[d]
        base_sum = base_sum + xbuf[d].astype(F32)
        kept_sum = kept_sum + lbuf[d].astype(F32)
    k = combine(k, lbuf)
    for copy in shares:
        copy.wait_recv()
    per = 128 // LISTED
    mine = iota((n_tm, 128), 1) // LISTED == lax.rem(iota((n_tm, 128), 0), per)
    spaced = jnp.where(mine, idbuf[...].reshape(n_tm, 128), 0.0).reshape(n_tm // per, per, 128)
    spaced = jnp.sum(spaced, axis=1, keepdims=True)
    key = jnp.concatenate([spaced[c] for c in range(n_tm // per)], axis=1)
    slot = det * n_tm + tm
    loads[9].wait()
    tile_mine = jnp.sum(
        jnp.where(owner[...] == slot, iota((1, 128), 1), 0).astype(F32), axis=1, keepdims=True
    )
    same = (own_key.astype(F32)[:, 0:1] == key).astype(F32).astype(BF16)
    into = (tile_mine * 128.0 + iota((128, listed), 0).astype(F32) == key).astype(F32).astype(BF16)
    all_squares = wbuf[...].reshape(listed, TILE)
    own_scale = 1.0 / (1.0 + squared_gain * jnp.dot(same, all_squares, preferred_element_type=F32))
    tile_weight = 1.0 + squared_gain * jnp.dot(into, all_squares, preferred_element_type=F32)
    tile_scale = jnp.sqrt(tile_weight) / tile_weight

    all_of(pbuf, p_recv, n_tm - 1)
    first = pbuf[...].reshape(listed, TILE)
    fetched = (jnp.dot(same, first, preferred_element_type=F32) * own_scale).astype(BF16)
    wide = jnp.dot(fetched, pt_t[...], preferred_element_type=F32)
    diagonal = iota((LISTED, LISTED * SEGLEN), 0) == iota((LISTED, LISTED * SEGLEN), 1) // SEGLEN
    flat = jnp.sum(jnp.where(diagonal, wide, 0.0), axis=0, keepdims=True)
    parts = []
    for s in range(SEG_DEV):
        total = flat[:, s * KBLK * SEGLEN : (s * KBLK + 1) * SEGLEN]
        for n in range(s * KBLK + 1, (s + 1) * KBLK):
            total = total + flat[:, n * SEGLEN : (n + 1) * SEGLEN]
        parts.append(total)
    sig = jnp.concatenate(parts, axis=1)
    qbuf[0] = project(filter_rows(r - sig * k)[0:1]).astype(BF16)
    spread_rows(qbuf, q_send, q_recv, (0, 1, 3, 2))

    amp = filter_rows(base_sum - sig * kept_sum)
    amp_high = amp.astype(BF16).astype(F32)
    amp_cat = jnp.concatenate([amp_high, amp_high, amp - amp_high, jnp.zeros_like(amp)], axis=0).astype(BF16)
    chunk = 128

    def clean_rows(c, carry):
        at = pl.ds(pl.multiple_of(c * chunk, chunk), chunk)
        gains_here = jnp.concatenate([gcol[at, :]] * (FLEN // 128), axis=1)
        left = ((ts[at, :] - gains_here * sig) * keepb[at, :].astype(F32)).astype(BF16)
        shaped = (jnp.dot(left, table[...], preferred_element_type=F32) * response).astype(BF16)
        filtered = jnp.dot(shaped, table_t[...], preferred_element_type=F32)
        filtered = filtered - jnp.dot(vcat[at, :], amp_cat, preferred_element_type=F32)
        clean[at, :] = filtered.astype(BF16)
        return carry

    lax.fori_loop(0, ts.shape[0] // chunk, clean_rows, 0)
    sums = jnp.dot(into, first, preferred_element_type=F32)

    all_of(qbuf, q_recv, n_tm - 1)
    second = qbuf[...].reshape(listed, TILE)
    sums = sums + jnp.dot(into, second, preferred_element_type=F32)
    tile_out[...] = sums * tile_scale

    for buf, sem in ((xbuf, x_send), (ybuf, y_send), (lbuf, l_send), (kbuf, k_send)):
        all_of(buf, sem, n_det - 1)
    for copy in shares:
        copy.wait_send()
    all_of(wbuf, w_send, half - 1)
    all_of(idbuf, id_send, half - 1)
    all_of(pbuf, p_send, n_tm - 1)
    all_of(qbuf, q_send, n_tm - 1)


def hand_out(tile, clean, tile_hbm, clean_hbm, sem):
    copies = [pltpu.make_async_copy(tile, tile_hbm, sem.at[0]), pltpu.make_async_copy(clean, clean_hbm, sem.at[1])]
    for copy in copies:
        copy.start()
    for copy in copies:
        copy.wait()


def solution(mesh):
    n_det, n_tm = mesh.shape["det"], mesh.shape["tm"]
    table_const = half_table()

    def shards(
        timestream, sample_flags, pointing, tile_ids, block_offsets, tile_owner, det_gains, mode_vectors, filter_gain
    ):
        dets, samples = timestream.shape
        hbm = pl.BlockSpec(memory_space=pltpu.HBM)
        vmem = pl.BlockSpec(memory_space=pltpu.VMEM)
        dma = pltpu.SemaphoreType.DMA
        tile_snr, cleaned = pl.pallas_call(
            functools.partial(kernel, n_det, n_tm),
            out_shape=(
                jax.ShapeDtypeStruct((TILE, TILE), F32),
                jax.ShapeDtypeStruct((dets, samples), BF16),
            ),
            in_specs=[hbm] * 10,
            out_specs=(vmem, vmem),
            scratch_shapes=[
                pltpu.VMEM((1, dets), F32),
                pltpu.VMEM((MODES, dets), F32),
                pltpu.VMEM((dets, samples), jnp.int32),
                pltpu.VMEM((dets, samples), F32),
                pltpu.VMEM((LISTED * SEGLEN, TILE), BF16),
                pltpu.SMEM((SEG_DEV, KBLK), jnp.int32),
                pltpu.SMEM((SEG_DEV, KBLK), jnp.int32),
                pltpu.VMEM((FLEN, FLEN), BF16),
                pltpu.VMEM((HALF + 1,), F32),
                pltpu.VMEM((1, tile_owner.shape[0]), jnp.int32),
                pltpu.VMEM((dets, samples), BF16),
                pltpu.VMEM((dets, 128), F32),
                pltpu.VMEM((dets, 128), BF16),
                pltpu.VMEM((FLEN, FLEN), BF16),
                pltpu.VMEM((TILE, LISTED * SEGLEN), BF16),
                pltpu.VMEM((FLEN, 2 * FLEN), BF16),
                pltpu.VMEM((n_det, 2, samples), F32),
                pltpu.VMEM((n_det, MODES, samples), BF16),
                pltpu.VMEM((n_det, MODES, samples), BF16),
                pltpu.VMEM((n_det, 1, samples), F32),
                pltpu.VMEM((n_tm, LISTED, TILE), BF16),
                pltpu.VMEM((n_tm, 1, 128), F32),
                pltpu.VMEM((n_tm, LISTED, TILE), BF16),
                pltpu.VMEM((n_tm, LISTED, TILE), BF16),
                pltpu.SemaphoreType.REGULAR,
                pltpu.SemaphoreType.REGULAR,
                dma((2,)),
                dma((2,)),
                dma((10,)),
            ]
            + [dma] * 16,
            compiler_params=pltpu.CompilerParams(
                collective_id=0, has_side_effects=True, vmem_limit_bytes=40 * 1024 * 1024
            ),
        )(
            *(
                pltpu.with_memory_space_constraint(operand, pltpu.HBM)
                for operand in (
                    det_gains.reshape(1, -1),
                    mode_vectors.T,
                    sample_flags,
                    timestream,
                    pointing.reshape(LISTED * SEGLEN, TILE),
                    tile_ids,
                    block_offsets,
                    jnp.asarray(table_const),
                    filter_gain,
                    tile_owner.reshape(1, -1),
                )
            )
        )
        tile_snr, cleaned = pl.pallas_call(
            hand_out,
            out_shape=(
                jax.ShapeDtypeStruct((TILE, TILE), F32),
                jax.ShapeDtypeStruct((dets, samples), BF16),
            ),
            in_specs=[vmem, vmem],
            out_specs=(hbm, hbm),
            scratch_shapes=[dma((2,))],
        )(*(pltpu.with_memory_space_constraint(x, pltpu.VMEM) for x in (tile_snr, cleaned)))
        return tile_snr.reshape(1, TILE, TILE), cleaned

    return jax.shard_map(
        shards,
        mesh=mesh,
        in_specs=(
            P("det", "tm"), P("det", "tm"), P("tm", None, None, None), P("tm", None), P("tm", None),
            P(), P("det"), P("det", None), P(),
        ),
        out_specs=(P(("det", "tm"), None, None), P("det", "tm")),
        check_vma=False,
    )
```
